128 devices in a mesh: fsdp: 16 (over z, y), tensor: 8 (over x, core).
Axes of the slice: x: 4, y: 4, z: 4, core: 2. Of those that a mesh axis runs over, the one named last changes fastest.
Arguments:
- momentum: float32 [8192, 26624], P('fsdp', 'tensor'), may hold values from -180 to 180
- gradient: bfloat16 [8192, 26624], P('fsdp', 'tensor'), may hold values from -180 to 180
- factor: float32 [26624, 128], P('tensor'), may hold values from -1 to 1
Outputs:
- new_momentum: float32 [8192, 26624], P('fsdp', 'tensor')
- left_basis: float32 [8192, 128], P('fsdp')
- new_factor: float32 [26624, 128], P('tensor')
The draws below stay inside these ranges and needn't reach their ends.
All inputs are finite; a program needn't handle non-finite values.
Results may differ from the reference program's by a relative error of at most 0.0003.
Values sent between devices are 32-bit elements; how exact they have to be, the bound alone decides.
A program may use at most 64 MiB of HBM per device.

```python
import jax
import jax.numpy as jnp
from jax import lax

D = 8192
FF = 26624
RANK = 128


def shared_scales(key):
    row_key = jax.random.fold_in(key, 11)
    col_key = jax.random.fold_in(key, 12)
    row_position = jnp.arange(D, dtype=jnp.float32) / D
    col_position = jnp.arange(FF, dtype=jnp.float32) / FF
    row_log = jnp.log(3.0) * row_position + jax.random.uniform(row_key, (D,), jnp.float32, 0.0, jnp.log(10.0))
    col_log = jnp.log(3.0) * col_position + jax.random.uniform(col_key, (FF,), jnp.float32, 0.0, jnp.log(10.0))
    row_scale = jnp.exp(row_log - 0.5 * jnp.log(30.0))
    col_scale = jnp.exp(col_log - 0.5 * jnp.log(30.0))
    return (row_scale[:, None], col_scale[None, :])


def scaled_noise(key, row_scale, col_scale):
    noise_draw = jnp.clip(jax.random.normal(key, (D, FF), jnp.float32), -6.0, 6.0)
    return noise_draw * row_scale * col_scale


def draw_momentum(key, part):
    row_scale, col_scale = shared_scales(key)
    key = jax.random.fold_in(key, 1)
    return scaled_noise(key, row_scale, col_scale)


def draw_gradient(key, part):
    row_scale, col_scale = shared_scales(key)
    key = jax.random.fold_in(key, 2)
    return scaled_noise(key, row_scale, col_scale).astype(jnp.bfloat16)


def draw_factor(key, part):
    key = jax.random.fold_in(key, 3)
    common_key = jax.random.fold_in(key, 21)
    weight_key = jax.random.fold_in(key, 22)
    spread_key = jax.random.fold_in(key, 23)
    common = jnp.clip(jax.random.normal(common_key, (FF, 1), jnp.float32), -6.0, 6.0)
    column_weight = jax.random.uniform(weight_key, (1, RANK), jnp.float32, 0.7, 1.3)
    spread = jnp.clip(jax.random.normal(spread_key, (FF, RANK), jnp.float32), -6.0, 6.0)
    spread_size = jnp.sqrt(RANK * 1.0) / 750.0
    return (common * column_weight + spread_size * spread) / jnp.sqrt(FF * 1.0)


def setup_inputs(seed: int = 0) -> dict:
    streams_of = jax.random.split(jax.random.key(seed), 4)
    momentum = draw_momentum(jax.random.fold_in(streams_of[3], 71), 0)
    gradient = draw_gradient(jax.random.fold_in(streams_of[3], 71), 0)
    factor = draw_factor(jax.random.fold_in(streams_of[3], 71), 0)
    return dict(momentum=momentum, gradient=gradient, factor=factor)


highest = lax.Precision.HIGHEST
momentum_decay = 0.9

def matmul(left_side, right_side):
    return jnp.dot(left_side.astype(jnp.float32), right_side.astype(jnp.float32), precision=highest, preferred_element_type=jnp.float32)

def contract_rows(left_side, right_side):
    return lax.dot_general(left_side.astype(jnp.float32), right_side.astype(jnp.float32), (((0,), (0,)), ((), ())), precision=highest, preferred_element_type=jnp.float32)

def orthonormal_pass(left_rows, gram_matrix):
    lower_factor = jnp.linalg.cholesky(gram_matrix)
    return lax.linalg.triangular_solve(lower_factor, left_rows, left_side=False, lower=True, transpose_a=True)

def reference(momentum, gradient, factor):
    summed = momentum + gradient.astype(jnp.float32)
    left_rows = matmul(summed, factor)
    for repeat in range(2):
        gram_matrix = contract_rows(left_rows, left_rows)
        left_rows = orthonormal_pass(left_rows, gram_matrix)
    right_factor = contract_rows(summed, left_rows)
    squares = lax.optimization_barrier(jnp.sum(right_factor * right_factor, axis=0))
    new_factor = right_factor * lax.rsqrt(squares + 1e-06)
    new_momentum = summed - (1.0 - momentum_decay) * matmul(left_rows, right_factor.T)
    return (new_momentum, left_rows, new_factor)
```

```python
import jax
import jax.numpy as jnp
from jax import lax
from jax.experimental import pallas as pl
from jax.experimental.pallas import tpu as pltpu
from jax.sharding import PartitionSpec as P

MESH = pl.DeviceIdType.MESH
HIGHEST = lax.Precision.HIGHEST
f32, bf16 = jnp.float32, jnp.bfloat16
momentum_decay = 0.9

ROWS, COLS, RANK = 512, 3328, 128
FSDP, TENSOR, SIDE = 16, 8, 4
CHUNKS = 4
CHUNK = ROWS // CHUNKS
HALF = COLS // 2
WIDE = 256
PANEL = 16


def dot(left, right, precision=None):
    return jnp.dot(left, right, precision=precision, preferred_element_type=f32)


def dot_rows(left, right, precision=None):
    return lax.dot_general(left, right, (((0,), (0,)), ((), ())), precision=precision, preferred_element_type=f32)


def dot_lanes(left, right, precision=None):
    return lax.dot_general(left, right, (((1,), (1,)), ((), ())), precision=precision, preferred_element_type=f32)


def split3(x):
    first = x.astype(bf16)
    rest = x - first.astype(f32)
    second = rest.astype(bf16)
    third = (rest - second.astype(f32)).astype(bf16)
    return first, second, third


def split2(x):
    first = x.astype(bf16)
    return first, (x - first.astype(f32)).astype(bf16)


def tiles(width, step=WIDE):
    return [(at, min(step, width - at)) for at in range(0, width, step)]


def factor_panel(work, start):
    shape = (PANEL, RANK)
    row = lax.broadcasted_iota(jnp.int32, shape, 0)
    lane = lax.broadcasted_iota(jnp.int32, shape, 1)
    panel = work[start : start + PANEL, :]
    column = [jnp.broadcast_to(panel[:, start + m : start + m + 1], shape) for m in range(PANEL)]
    left, right = panel[:, :RANK], panel[:, RANK:]
    scale = jnp.zeros(shape, f32)
    for i in range(PANEL):
        pivot = jnp.broadcast_to(column[i][i : i + 1, :], shape)
        scale = jnp.where(row == i, lax.rsqrt(pivot), scale)
        if i < PANEL - 1:
            ratio = jnp.where(row > i, column[i] * (1.0 / pivot), 0.0)
            for m in range(i + 1, PANEL):
                column[m] = column[m] - ratio * column[m][i : i + 1, :]
            left = left - ratio * left[i : i + 1, :]
            right = right - ratio * right[i : i + 1, :]
    left, right = left * scale, right * scale
    both = jnp.concatenate([left, right], axis=1)
    work[start : start + PANEL, :] = both
    below = start + PANEL
    if below < RANK:
        update = dot_rows(jnp.where(lane >= below, left, 0.0), both, HIGHEST)
        work[below:, :] = work[below:, :] - update[below:, :]


def cholesky_inverse(work, gram, between=()):
    row = lax.broadcasted_iota(jnp.int32, (RANK, RANK), 0)
    lane = lax.broadcasted_iota(jnp.int32, (RANK, RANK), 1)
    work[:, :RANK] = gram
    work[:, RANK:] = jnp.where(row == lane, 1.0, 0.0)
    for k in range(RANK // PANEL):
        factor_panel(work, k * PANEL)
        if k in between:
            between[k]()
    return work[:, RANK:]


def kernel(
    momentum, gradient, factor, new_momentum, left_basis, new_factor,
    summed, grad, fac, s1, s2, s3, f12, f31, part, core_in, cross, a_full, grams, gram_all, work, bt, rt, rsa, rsb, squares, gram_part,
    load_sem, a_send, a_recv, g_send, g_recv, r_send, r_recv,
):
    f, t = lax.axis_index("fsdp"), lax.axis_index("tensor")
    z, y = f // SIDE, lax.rem(f, SIDE)
    x, c = t // 2, lax.rem(t, 2)
    other_core = (f, x * 2 + 1 - c)
    x_peers = [(f, lax.rem(x + k, SIDE) * 2 + c) for k in range(1, SIDE)]
    t_peers = [(f, lax.rem(t + k, TENSOR)) for k in range(1, TENSOR)]
    f_peers = [(lax.rem(f + k, FSDP), t) for k in range(1, FSDP)]
    along = {
        "y": (y, [lax.rem(y + k, SIDE) for k in range(1, SIDE)], lambda v: (z * SIDE + v, t)),
        "z": (z, [lax.rem(z + k, SIDE) for k in range(1, SIDE)], lambda v: (v * SIDE + y, t)),
    }

    def remote(src, dst, send, recv, to):
        copy = pltpu.make_async_remote_copy(
            src_ref=src, dst_ref=dst, send_sem=send, recv_sem=recv, device_id=to, device_id_type=MESH
        )
        copy.start()
        return copy

    loads = [pltpu.make_async_copy(factor, fac, load_sem.at[2 * CHUNKS])]
    for i in range(CHUNKS):
        rows = pl.ds(i * CHUNK, CHUNK)
        loads.append(pltpu.make_async_copy(momentum.at[rows], summed.at[rows], load_sem.at[2 * i]))
        loads.append(pltpu.make_async_copy(gradient.at[rows], grad.at[rows], load_sem.at[2 * i + 1]))
    for load in loads:
        load.start()

    barrier = pltpu.get_barrier_semaphore()
    greeted = t_peers + f_peers
    for peer in greeted:
        pl.semaphore_signal(barrier, inc=1, device_id=peer, device_id_type=MESH)

    loads[0].wait()
    first, second, third = split3(fac[...])
    f12[:, :RANK], f12[:, RANK:] = first, second
    f31[:COLS, :], f31[COLS:, :] = third, first

    half = CHUNK // 2
    core_copies, cross_copies, back_copies = [], [], []

    def pass_across(i):
        core_copies[i].wait_recv()
        cross[i, x] = part[i, pl.ds(c * half, half)] + core_in[i]
        cross_copies.append(
            [
                remote(cross.at[i, x], cross.at[i, x], a_send.at[CHUNKS + 3 * i + k], a_recv.at[CHUNKS + 3 * i + k], peer)
                for k, peer in enumerate(x_peers)
            ]
        )

    def pass_back(i):
        for copy in cross_copies[i]:
            copy.wait_recv()
        mine = pl.ds(i * CHUNK + c * half, half)
        a_full[mine, :] = (cross[i, 0] + cross[i, 1]) + (cross[i, 2] + cross[i, 3])
        back_copies.append(
            remote(a_full.at[mine], a_full.at[mine], a_send.at[4 * CHUNKS + i], a_recv.at[4 * CHUNKS + i], other_core)
        )

    for i in range(CHUNKS):
        rows = pl.ds(i * CHUNK, CHUNK)
        loads[1 + 2 * i].wait()
        loads[2 + 2 * i].wait()

        def add_and_split(j, carry):
            at = (rows, pl.ds(pl.multiple_of(j * WIDE, WIDE), WIDE))
            total = summed[at] + grad[at].astype(f32)
            summed[at] = total
            s1[at], s2[at], s3[at] = split3(total)
            return carry

        lax.fori_loop(0, COLS // WIDE, add_and_split, 0)
        pair = dot(s1[rows, :], f12[...]) + dot(s2[rows, :], f12[...])
        small = dot(s1[rows, :], f31[:COLS, :]) + dot(s3[rows, :], f31[COLS:, :])
        part[i] = pair[:, :RANK] + (pair[:, RANK:] + small)
        if i == 0:
            pl.semaphore_wait(barrier, len(greeted))
        core_copies.append(
            remote(part.at[i, pl.ds((1 - c) * half, half)], core_in.at[i], a_send.at[i], a_recv.at[i], other_core)
        )
        if i > 0:
            pass_across(i - 1)
    pass_across(CHUNKS - 1)
    for i in range(CHUNKS):
        pass_back(i)
    for i in range(CHUNKS):
        back_copies[i].wait_recv()

    def gram_send(k, rows):
        gram_part[...] = dot_rows(rows, rows, HIGHEST)
        share = RANK // TENSOR
        grams[k, f] = gram_part[pl.ds(pl.multiple_of(t * share, share), share), :]
        return [
            remote(grams.at[k, f], grams.at[k, f], g_send.at[k, n], g_recv.at[k, n], peer) for n, peer in enumerate(f_peers)
        ]

    def gram_share(k, copies):
        for copy in copies:
            copy.wait_recv()
        total = grams[k, 0]
        for n in range(1, FSDP):
            total = total + grams[k, n]
        gram_all[k, t] = total
        return [
            remote(gram_all.at[k, t], gram_all.at[k, t], g_send.at[k, FSDP - 1 + n], g_recv.at[k, FSDP - 1 + n], peer)
            for n, peer in enumerate(t_peers)
        ]

    def gram_take(k, copies):
        for copy in copies:
            copy.wait_recv()
        return gram_all[k].reshape(RANK, RANK)

    a = a_full[...]
    started = []
    gram1 = gram_send(0, a)
    started += gram1

    at1, at2, at3 = split3(a.T)
    stack = jnp.concatenate([at1, at2, at3], axis=0)
    order = (("y", "z"), ("z", "y"))
    chunk_rows = RANK // SIDE
    piece_rows = chunk_rows // SIDE
    first_sends = []
    for h in range(2):
        for at, width in tiles(HALF):
            cols = pl.ds(h * HALF + at, width)
            one = dot(stack, s1[:, cols])
            two = dot(stack[: 2 * RANK], s2[:, cols])
            three = dot(at1, s3[:, cols])
            low = one[2 * RANK :] + (two[RANK:] + three)
            bt[h, :, at : at + width] = one[:RANK] + ((one[RANK : 2 * RANK] + two[:RANK]) + low)
        _, peers, where = along[order[h][0]]
        first_sends.append(
            [
                remote(
                    bt.at[h, pl.ds(v * chunk_rows, chunk_rows)], rsa.at[h, k], r_send.at[0, h, k], r_recv.at[0, h, k], where(v)
                )
                for k, v in enumerate(peers)
            ]
        )
    started += first_sends[0] + first_sends[1]

    share1 = gram_share(0, gram1)
    started += share1
    gram_one = gram_take(0, share1)
    inverse_one = cholesky_inverse(work, gram_one)
    second_left = dot_lanes(a, inverse_one, HIGHEST)
    gram2 = gram_send(1, second_left)
    started += gram2

    def place(h):
        own = along[order[h][0]][0] * chunk_rows
        return own, own + along[order[h][1]][0] * piece_rows

    second_sends = []
    for h in range(2):
        for copy in first_sends[h]:
            copy.wait_recv()
        own, _ = place(h)
        mine = pl.ds(pl.multiple_of(own, chunk_rows), chunk_rows)
        bt[h, mine] = (bt[h, mine] + rsa[h, 0]) + (rsa[h, 1] + rsa[h, 2])
        _, peers, where = along[order[h][1]]
        second_sends.append(
            [
                remote(
                    bt.at[h, pl.ds(own + v * piece_rows, piece_rows)],
                    rsb.at[h, k], r_send.at[1, h, k], r_recv.at[1, h, k], where(v),
                )
                for k, v in enumerate(peers)
            ]
        )
    started += second_sends[0] + second_sends[1]
    share2 = gram_share(1, gram2)
    started += share2

    third_sends = []
    for h in range(2):
        for copy in second_sends[h]:
            copy.wait_recv()
        _, at = place(h)
        mine = pl.ds(pl.multiple_of(at, piece_rows), piece_rows)
        rt[h, mine] = (bt[h, mine] + rsb[h, 0]) + (rsb[h, 1] + rsb[h, 2])
        _, peers, where = along[order[h][1]]
        third_sends.append(
            [
                remote(rt.at[h, mine], rt.at[h, mine], r_send.at[2, h, k], r_recv.at[2, h, k], where(v))
                for k, v in enumerate(peers)
            ]
        )
    started += third_sends[0] + third_sends[1]

    gram_two = gram_take(1, share2)
    fourth_sends = []

    def send_fourth():
        for h in range(2):
            for copy in third_sends[h]:
                copy.wait_recv()
            own, _ = place(h)
            mine = pl.ds(pl.multiple_of(own, chunk_rows), chunk_rows)
            _, peers, where = along[order[h][0]]
            fourth_sends.append(
                [
                    remote(rt.at[h, mine], rt.at[h, mine], r_send.at[3, h, k], r_recv.at[3, h, k], where(v))
                    for k, v in enumerate(peers)
                ]
            )

    inverse_two = cholesky_inverse(work, gram_two, {1: send_fourth})
    started += fourth_sends[0] + fourth_sends[1]
    basis = dot_lanes(second_left, inverse_two, HIGHEST)
    left_basis[...] = basis
    turn = dot(inverse_two, inverse_one, HIGHEST)
    q1, q2 = split2(basis * (1.0 - momentum_decay))
    q12 = jnp.concatenate([q1, q2], axis=1)

    local = jnp.zeros((1, RANK), f32)
    for h in range(2):
        for copy in fourth_sends[h]:
            copy.wait_recv()
        for at, width in tiles(HALF):
            cols = pl.ds(h * HALF + at, width)
            right = dot(turn, rt[h, :, at : at + width], HIGHEST)
            upright = right.T
            new_factor[cols, :] = upright
            local = local + jnp.sum(upright * upright, axis=0, keepdims=True)
            r1, r2 = split2(right)
            low = dot(q12, jnp.concatenate([r1, r1], axis=0)) + dot(q1, r2)
            new_momentum[:, cols] = summed[:, cols] - low
    squares[t] = jnp.broadcast_to(local, (8, RANK))
    last = [
        remote(squares.at[t], squares.at[t], a_send.at[5 * CHUNKS + n], a_recv.at[5 * CHUNKS + n], peer)
        for n, peer in enumerate(t_peers)
    ]
    for copy in last:
        copy.wait_recv()
    total = squares[0]
    for n in range(1, TENSOR):
        total = total + squares[n]
    norm = lax.rsqrt(total[:1] + 1e-06)
    new_factor[...] = new_factor[...] * norm
    for copies in cross_copies:
        started += copies
    for copy in started + core_copies + back_copies + last:
        copy.wait_send()


def per_device(momentum, gradient, factor):
    dma = pltpu.SemaphoreType.DMA
    return pl.pallas_call(
        kernel,
        out_shape=(
            jax.ShapeDtypeStruct((ROWS, COLS), f32),
            jax.ShapeDtypeStruct((ROWS, RANK), f32),
            jax.ShapeDtypeStruct((COLS, RANK), f32),
        ),
        in_specs=[pl.BlockSpec(memory_space=pl.ANY)] * 3,
        out_specs=[pl.BlockSpec(memory_space=pltpu.VMEM)] * 3,
        scratch_shapes=[
            pltpu.VMEM((ROWS, COLS), f32),
            pltpu.VMEM((ROWS, COLS), bf16),
            pltpu.VMEM((COLS, RANK), f32),
            pltpu.VMEM((ROWS, COLS), bf16),
            pltpu.VMEM((ROWS, COLS), bf16),
            pltpu.VMEM((ROWS, COLS), bf16),
            pltpu.VMEM((COLS, 2 * RANK), bf16),
            pltpu.VMEM((2 * COLS, RANK), bf16),
            pltpu.VMEM((CHUNKS, CHUNK, RANK), f32),
            pltpu.VMEM((CHUNKS, CHUNK // 2, RANK), f32),
            pltpu.VMEM((CHUNKS, SIDE, CHUNK // 2, RANK), f32),
            pltpu.VMEM((ROWS, RANK), f32),
            pltpu.VMEM((2, FSDP, RANK // TENSOR, RANK), f32),
            pltpu.VMEM((2, TENSOR, RANK // TENSOR, RANK), f32),
            pltpu.VMEM((RANK, 2 * RANK), f32),
            pltpu.VMEM((2, RANK, HALF), f32),
            pltpu.VMEM((2, RANK, HALF), f32),
            pltpu.VMEM((2, SIDE - 1, RANK // SIDE, HALF), f32),
            pltpu.VMEM((2, SIDE - 1, RANK // FSDP, HALF), f32),
            pltpu.VMEM((TENSOR, 8, RANK), f32),
            pltpu.VMEM((RANK, RANK), f32),
            dma((2 * CHUNKS + 1,)),
            dma((5 * CHUNKS + TENSOR - 1,)),
            dma((5 * CHUNKS + TENSOR - 1,)),
            dma((2, FSDP + TENSOR - 2)),
            dma((2, FSDP + TENSOR - 2)),
            dma((4, 2, SIDE - 1)),
            dma((4, 2, SIDE - 1)),
        ],
        compiler_params=pltpu.CompilerParams(collective_id=0, has_side_effects=True, vmem_limit_bytes=56 << 20),
        cost_estimate=pl.CostEstimate(flops=8 * 10**9, bytes_accessed=20 * 10**6, transcendentals=0),
        name="dion_update",
    )(momentum, gradient, factor)


def solution(mesh):
    return jax.shard_map(
        per_device,
        mesh=mesh,
        in_specs=(P("fsdp", "tensor"), P("fsdp", "tensor"), P("tensor", None)),
        out_specs=(P("fsdp", "tensor"), P("fsdp", None), P("tensor", None)),
        check_vma=False,
    )
```

```python
import jax
import jax.numpy as jnp
from jax import lax
from jax.experimental import pallas as pl
from jax.experimental.pallas import tpu as pltpu
from jax.sharding import PartitionSpec as P

MESH = pl.DeviceIdType.MESH
HIGHEST = lax.Precision.HIGHEST
f32, bf16 = jnp.float32, jnp.bfloat16
momentum_decay = 0.9

ROWS, COLS, RANK = 512, 3328, 128
FSDP, TENSOR, SIDE = 16, 8, 4
CHUNKS = 4
CHUNK = ROWS // CHUNKS
GROUPS = ((0, 896, "y", "z"), (896, 896, "z", "y"), (1792, 768, "y", "z"), (2560, 768, "z", "y"))
WIDE = 256
PANEL = 16


def dot(left, right, precision=None):
    return jnp.dot(left, right, precision=precision, preferred_element_type=f32)


def dot_rows(left, right, precision=None):
    return lax.dot_general(left, right, (((0,), (0,)), ((), ())), precision=precision, preferred_element_type=f32)


def dot_lanes(left, right, precision=None):
    return lax.dot_general(left, right, (((1,), (1,)), ((), ())), precision=precision, preferred_element_type=f32)


def split3(x):
    first = x.astype(bf16)
    rest = x - first.astype(f32)
    second = rest.astype(bf16)
    third = (rest - second.astype(f32)).astype(bf16)
    return first, second, third


def split2(x):
    first = x.astype(bf16)
    return first, (x - first.astype(f32)).astype(bf16)


def tiles(width, step=WIDE):
    return [(at, min(step, width - at)) for at in range(0, width, step)]


def factor_panel(work, start):
    shape = (PANEL, RANK)
    row = lax.broadcasted_iota(jnp.int32, shape, 0)
    lane = lax.broadcasted_iota(jnp.int32, shape, 1)
    panel = work[start : start + PANEL, :]
    column = [jnp.broadcast_to(panel[:, start + m : start + m + 1], shape) for m in range(PANEL)]
    left, right = panel[:, :RANK], panel[:, RANK:]
    scale = jnp.zeros(shape, f32)
    for i in range(PANEL):
        pivot = jnp.broadcast_to(column[i][i : i + 1, :], shape)
        scale = jnp.where(row == i, lax.rsqrt(pivot), scale)
        if i < PANEL - 1:
            ratio = jnp.where(row > i, column[i] * (1.0 / pivot), 0.0)
            for m in range(i + 1, PANEL):
                column[m] = column[m] - ratio * column[m][i : i + 1, :]
            left = left - ratio * left[i : i + 1, :]
            right = right - ratio * right[i : i + 1, :]
    left, right = left * scale, right * scale
    both = jnp.concatenate([left, right], axis=1)
    work[start : start + PANEL, :] = both
    below = start + PANEL
    if below < RANK:
        update = dot_rows(jnp.where(lane >= below, left, 0.0), both, HIGHEST)
        work[below:, :] = work[below:, :] - update[below:, :]


def cholesky_inverse(work, gram, between=()):
    row = lax.broadcasted_iota(jnp.int32, (RANK, RANK), 0)
    lane = lax.broadcasted_iota(jnp.int32, (RANK, RANK), 1)
    work[:, :RANK] = gram
    work[:, RANK:] = jnp.where(row == lane, 1.0, 0.0)
    for k in range(RANK // PANEL):
        factor_panel(work, k * PANEL)
        if k in between:
            between[k]()
    return work[:, RANK:]


def kernel(
    momentum, gradient, factor, summed, left_basis, new_factor,
    grad, fac, s1, s2, s3, f12, f3, part, core_in, cross, a_full, grams, gram_all, gram_part, work, bt, rt, rsa, rsb,
    squares, right_rows,
    load_sem, a_send, a_recv, g_send, g_recv, r_send, r_recv,
):
    f, t = lax.axis_index("fsdp"), lax.axis_index("tensor")
    z, y = f // SIDE, lax.rem(f, SIDE)
    x, c = t // 2, lax.rem(t, 2)
    other_core = (f, x * 2 + 1 - c)
    x_peers = [(f, lax.rem(x + k, SIDE) * 2 + c) for k in range(1, SIDE)]
    t_peers = [(f, lax.rem(t + k, TENSOR)) for k in range(1, TENSOR)]
    f_peers = [(lax.rem(f + k, FSDP), t) for k in range(1, FSDP)]
    along = {
        "y": (y, [lax.rem(y + k, SIDE) for k in range(1, SIDE)], lambda v: (z * SIDE + v, t)),
        "z": (z, [lax.rem(z + k, SIDE) for k in range(1, SIDE)], lambda v: (v * SIDE + y, t)),
    }
    sent = []

    def remote(src, dst, send, recv, to):
        copy = pltpu.make_async_remote_copy(
            src_ref=src, dst_ref=dst, send_sem=send, recv_sem=recv, device_id=to, device_id_type=MESH
        )
        copy.start()
        sent.append(copy)
        return copy

    loads = [pltpu.make_async_copy(factor, fac, load_sem.at[2 * CHUNKS])]
    for i in range(CHUNKS):
        rows = pl.ds(i * CHUNK, CHUNK)
        loads.append(pltpu.make_async_copy(momentum.at[rows], summed.at[rows], load_sem.at[2 * i]))
        loads.append(pltpu.make_async_copy(gradient.at[rows], grad.at[rows], load_sem.at[2 * i + 1]))
    for load in loads:
        load.start()

    barrier = pltpu.get_barrier_semaphore()
    greeted = t_peers + f_peers
    for peer in greeted:
        pl.semaphore_signal(barrier, inc=1, device_id=peer, device_id_type=MESH)

    def add_and_split(i, at, width):
        where = (pl.ds(i * CHUNK, CHUNK), pl.ds(at, width))
        total = summed[where] + grad[where].astype(f32)
        summed[where] = total
        s1[where], s2[where], s3[where] = split3(total)

    def wait_rows(i):
        loads[1 + 2 * i].wait()
        loads[2 + 2 * i].wait()

    loads[0].wait()
    for at, width in tiles(COLS):
        here = pl.ds(at, width)
        f12[here, :RANK], f12[here, RANK:], f3[here, :] = split3(fac[here, :])
    wait_rows(0)
    for at, width in tiles(COLS):
        add_and_split(0, at, width)

    half = CHUNK // 2
    core_copies, cross_copies, back_copies = [], [], []

    def pass_across(i):
        core_copies[i].wait_recv()
        cross[i, x] = part[i, pl.ds(c * half, half)] + core_in[i]
        cross_copies.append(
            [
                remote(cross.at[i, x], cross.at[i, x], a_send.at[CHUNKS + 3 * i + k], a_recv.at[CHUNKS + 3 * i + k], peer)
                for k, peer in enumerate(x_peers)
            ]
        )

    def pass_back(i):
        for copy in cross_copies[i]:
            copy.wait_recv()
        mine = pl.ds(i * CHUNK + c * half, half)
        a_full[mine, :] = (cross[i, 0] + cross[i, 1]) + (cross[i, 2] + cross[i, 3])
        back_copies.append(
            remote(a_full.at[mine], a_full.at[mine], a_send.at[4 * CHUNKS + i], a_recv.at[4 * CHUNKS + i], other_core)
        )

    for i in range(CHUNKS):
        rows = pl.ds(i * CHUNK, CHUNK)
        if i + 1 < CHUNKS:
            wait_rows(i + 1)
        pair = jnp.zeros((CHUNK, 2 * RANK), f32)
        small = jnp.zeros((CHUNK, RANK), f32)
        for at, width in tiles(COLS):
            if i + 1 < CHUNKS:
                add_and_split(i + 1, at, width)
            here = pl.ds(at, width)
            pair = pair + (dot(s1[rows, here], f12[here, :]) + dot(s2[rows, here], f12[here, :]))
            small = small + (dot(s1[rows, here], f3[here, :]) + dot(s3[rows, here], f12[here, :RANK]))
        part[i] = pair[:, :RANK] + (pair[:, RANK:] + small)
        if i == 0:
            pl.semaphore_wait(barrier, len(greeted))
        core_copies.append(
            remote(part.at[i, pl.ds((1 - c) * half, half)], core_in.at[i], a_send.at[i], a_recv.at[i], other_core)
        )
        if i > 0:
            pass_across(i - 1)
    pass_across(CHUNKS - 1)
    for i in range(CHUNKS):
        pass_back(i)
    for copy in back_copies:
        copy.wait_recv()

    def gram_send(k, rows):
        gram_part[...] = dot_rows(rows, rows, HIGHEST)
        share = RANK // TENSOR
        grams[k, f] = gram_part[pl.ds(pl.multiple_of(t * share, share), share), :]
        return [
            remote(grams.at[k, f], grams.at[k, f], g_send.at[k, n], g_recv.at[k, n], peer) for n, peer in enumerate(f_peers)
        ]

    def gram_share(k, copies):
        for copy in copies:
            copy.wait_recv()
        total = grams[k, 0]
        for n in range(1, FSDP):
            total = total + grams[k, n]
        gram_all[k, t] = total
        return [
            remote(gram_all.at[k, t], gram_all.at[k, t], g_send.at[k, FSDP - 1 + n], g_recv.at[k, FSDP - 1 + n], peer)
            for n, peer in enumerate(t_peers)
        ]

    def gram_take(k, copies):
        for copy in copies:
            copy.wait_recv()
        return gram_all[k].reshape(RANK, RANK)

    a = a_full[...]
    gram1 = gram_send(0, a)

    at1, at2, at3 = split3(a.T)
    stack = jnp.concatenate([at1, at2, at3], axis=0)
    chunk_rows = RANK // SIDE
    piece_rows = chunk_rows // SIDE
    moves = {}

    def cols_of(g):
        return pl.ds(GROUPS[g][0], GROUPS[g][1])

    def place(g):
        own = pl.multiple_of(along[GROUPS[g][2]][0] * chunk_rows, chunk_rows)
        return own, pl.multiple_of(own + along[GROUPS[g][3]][0] * piece_rows, piece_rows)

    def multiply(g):
        start, size, _, _ = GROUPS[g]
        for at, width in tiles(size):
            cols = pl.ds(start + at, width)
            one = dot(stack, s1[:, cols])
            two = dot(stack[: 2 * RANK], s2[:, cols])
            three = dot(at1, s3[:, cols])
            low = one[2 * RANK :] + (two[RANK:] + three)
            bt[:, cols] = one[:RANK] + ((one[RANK : 2 * RANK] + two[:RANK]) + low)

    def first_send(g):
        _, peers, where = along[GROUPS[g][2]]
        cols = cols_of(g)
        moves[0, g] = [
            remote(
                bt.at[pl.ds(v * chunk_rows, chunk_rows), cols], rsa.at[k, :, cols], r_send.at[0, g, k], r_recv.at[0, g, k], where(v)
            )
            for k, v in enumerate(peers)
        ]

    def second_send(g):
        for copy in moves[0, g]:
            copy.wait_recv()
        own, _ = place(g)
        cols = cols_of(g)
        mine = pl.ds(own, chunk_rows)
        bt[mine, cols] = (bt[mine, cols] + rsa[0, :, cols]) + (rsa[1, :, cols] + rsa[2, :, cols])
        _, peers, where = along[GROUPS[g][3]]
        moves[1, g] = [
            remote(
                bt.at[pl.ds(own + v * piece_rows, piece_rows), cols],
                rsb.at[k, :, cols], r_send.at[1, g, k], r_recv.at[1, g, k], where(v),
            )
            for k, v in enumerate(peers)
        ]

    def third_send(g):
        for copy in moves[1, g]:
            copy.wait_recv()
        _, at = place(g)
        cols = cols_of(g)
        mine = pl.ds(at, piece_rows)
        rt[mine, cols] = (bt[mine, cols] + rsb[0, :, cols]) + (rsb[1, :, cols] + rsb[2, :, cols])
        _, peers, where = along[GROUPS[g][3]]
        moves[2, g] = [
            remote(rt.at[mine, cols], rt.at[mine, cols], r_send.at[2, g, k], r_recv.at[2, g, k], where(v))
            for k, v in enumerate(peers)
        ]

    def fourth_send(g):
        for copy in moves[2, g]:
            copy.wait_recv()
        own, _ = place(g)
        cols = cols_of(g)
        mine = pl.ds(own, chunk_rows)
        _, peers, where = along[GROUPS[g][2]]
        moves[3, g] = [
            remote(rt.at[mine, cols], rt.at[mine, cols], r_send.at[3, g, k], r_recv.at[3, g, k], where(v))
            for k, v in enumerate(peers)
        ]

    def both(step, *groups):
        def run():
            for g in groups:
                step(g)

        return run

    multiply(0)
    first_send(0)
    multiply(1)
    first_send(1)
    multiply(2)
    multiply(3)
    share1 = gram_share(0, gram1)
    both(first_send, 2, 3)()
    gram_one = gram_take(0, share1)
    inverse_one = cholesky_inverse(work, gram_one, {2: both(second_send, 0, 1), 6: both(second_send, 2, 3)})
    second_left = dot_lanes(a, inverse_one, HIGHEST)
    gram2 = gram_send(1, second_left)
    both(third_send, 0, 1, 2, 3)()
    share2 = gram_share(1, gram2)
    both(fourth_send, 0, 1, 2, 3)()
    gram_two = gram_take(1, share2)
    inverse_two = cholesky_inverse(work, gram_two)
    turn = dot(inverse_two, inverse_one, HIGHEST)
    basis = dot_lanes(second_left, inverse_two, HIGHEST)
    left_basis[...] = basis
    q12 = jnp.concatenate(split2(basis * (1.0 - momentum_decay)), axis=1)
    t1, t2, t3 = split3(turn)
    t12 = jnp.concatenate([t1, t2], axis=1)
    t13 = jnp.concatenate([t1, t3], axis=1)
    energy = jnp.zeros((RANK, RANK), f32)
    for g, (start, size, _, _) in enumerate(GROUPS):
        for copy in moves[3, g]:
            copy.wait_recv()
        for at, width in tiles(size):
            cols = pl.ds(start + at, width)
            r1, r2, r3 = split3(rt[:, cols])
            right = dot(t12, jnp.concatenate([r1, r1], axis=0)) + (
                dot(t12, jnp.concatenate([r2, r2], axis=0)) + dot(t13, jnp.concatenate([r3, r1], axis=0))
            )
            right_rows[:, cols] = right
            for lane in range(0, width, RANK):
                tile = right[:, lane : lane + RANK]
                energy = energy + tile * tile
    squares[t] = dot_lanes(jnp.ones((8, RANK), f32), energy, HIGHEST)
    last = [
        remote(squares.at[t], squares.at[t], a_send.at[5 * CHUNKS + n], a_recv.at[5 * CHUNKS + n], peer)
        for n, peer in enumerate(t_peers)
    ]
    for n, (start, size, _, _) in enumerate(GROUPS):
        for at, width in tiles(size):
            cols = pl.ds(start + at, width)
            right = right_rows[:, cols]
            rounded = right.astype(bf16)
            summed[:, cols] = summed[:, cols] - dot(q12, jnp.concatenate([rounded, rounded], axis=0))
            new_factor[cols, :] = right.T
    for copy in last:
        copy.wait_recv()
    total = squares[0]
    for n in range(1, TENSOR):
        total = total + squares[n]
    new_factor[...] = new_factor[...] * lax.rsqrt(total[:1] + 1e-06)
    for copy in sent:
        copy.wait_send()


def per_device(momentum, gradient, factor):
    dma = pltpu.SemaphoreType.DMA
    return pl.pallas_call(
        kernel,
        out_shape=(
            pltpu.VMEM((ROWS, COLS), f32),
            pltpu.VMEM((ROWS, RANK), f32),
            pltpu.VMEM((COLS, RANK), f32),
        ),
        in_specs=[pl.BlockSpec(memory_space=pltpu.HBM)] * 3,
        out_specs=[pl.BlockSpec(memory_space=pltpu.VMEM)] * 3,
        scratch_shapes=[
            pltpu.VMEM((ROWS, COLS), bf16),
            pltpu.VMEM((COLS, RANK), f32),
            pltpu.VMEM((ROWS, COLS), bf16),
            pltpu.VMEM((ROWS, COLS), bf16),
            pltpu.VMEM((ROWS, COLS), bf16),
            pltpu.VMEM((COLS, 2 * RANK), bf16),
            pltpu.VMEM((COLS, RANK), bf16),
            pltpu.VMEM((CHUNKS, CHUNK, RANK), f32),
            pltpu.VMEM((CHUNKS, CHUNK // 2, RANK), f32),
            pltpu.VMEM((CHUNKS, SIDE, CHUNK // 2, RANK), f32),
            pltpu.VMEM((ROWS, RANK), f32),
            pltpu.VMEM((2, FSDP, RANK // TENSOR, RANK), f32),
            pltpu.VMEM((2, TENSOR, RANK // TENSOR, RANK), f32),
            pltpu.VMEM((RANK, RANK), f32),
            pltpu.VMEM((RANK, 2 * RANK), f32),
            pltpu.VMEM((RANK, COLS), f32),
            pltpu.VMEM((RANK, COLS), f32),
            pltpu.VMEM((SIDE - 1, RANK // SIDE, COLS), f32),
            pltpu.VMEM((SIDE - 1, RANK // FSDP, COLS), f32),
            pltpu.VMEM((TENSOR, 8, RANK), f32),
            pltpu.VMEM((RANK, COLS), f32),
            dma((2 * CHUNKS + 1,)),
            dma((5 * CHUNKS + TENSOR - 1,)),
            dma((5 * CHUNKS + TENSOR - 1,)),
            dma((2, FSDP + TENSOR - 2)),
            dma((2, FSDP + TENSOR - 2)),
            dma((4, len(GROUPS), SIDE - 1)),
            dma((4, len(GROUPS), SIDE - 1)),
        ],
        compiler_params=pltpu.CompilerParams(collective_id=0, has_side_effects=True, vmem_limit_bytes=44 << 20),
        cost_estimate=pl.CostEstimate(flops=8 * 10**9, bytes_accessed=20 * 10**6, transcendentals=0),
        name="dion_update",
    )(*(pltpu.with_memory_space_constraint(v, pltpu.HBM) for v in (momentum, gradient, factor)))


def solution(mesh):
    return jax.shard_map(
        per_device,
        mesh=mesh,
        in_specs=(P("fsdp", "tensor"), P("fsdp", "tensor"), P("tensor", None)),
        out_specs=(P("fsdp", "tensor"), P("fsdp", None), P("tensor", None)),
        check_vma=False,
    )
```

```python
import jax
import jax.numpy as jnp
from jax import lax
from jax.experimental import pallas as pl
from jax.experimental.pallas import tpu as pltpu
from jax.sharding import PartitionSpec as P

MESH = pl.DeviceIdType.MESH
HIGHEST = lax.Precision.HIGHEST
f32, bf16 = jnp.float32, jnp.bfloat16
momentum_decay = 0.9

ROWS, COLS, RANK = 512, 3328, 128
FSDP, TENSOR, SIDE = 16, 8, 4
CHUNKS = 4
CHUNK = ROWS // CHUNKS
GROUPS = ((0, 896, "y", "z"), (896, 896, "z", "y"), (1792, 768, "y", "z"), (2560, 768, "z", "y"))
WIDE = 256
PANEL, STRIP = 64, 16
PLAN = (
    "gram1 m0 f0 m1", "f1 m2 m3 share1", "f2 f3 take1", "chol1:0=s0,0=s1", "gram2 s2 s3 t0", "t1 t2 t3 q0", "q1 share2 q2 q3",
    "take2 chol2",
)


def dot(left, right, precision=None):
    return jnp.dot(left, right, precision=precision, preferred_element_type=f32)


def dot_rows(left, right, precision=None):
    return lax.dot_general(left, right, (((0,), (0,)), ((), ())), precision=precision, preferred_element_type=f32)


def dot_lanes(left, right, precision=None):
    return lax.dot_general(left, right, (((1,), (1,)), ((), ())), precision=precision, preferred_element_type=f32)


def split3(x):
    first = x.astype(bf16)
    rest = x - first.astype(f32)
    second = rest.astype(bf16)
    third = (rest - second.astype(f32)).astype(bf16)
    return first, second, third


def split2(x):
    first = x.astype(bf16)
    return first, (x - first.astype(f32)).astype(bf16)


def tiles(width, step=WIDE):
    return [(at, min(step, width - at)) for at in range(0, width, step)]


def cholesky_inverse(work, gram, between):
    row = lax.broadcasted_iota(jnp.int32, (8, RANK), 0)
    spread = lambda x: jnp.broadcast_to(x, (8, RANK))
    row_all = lax.broadcasted_iota(jnp.int32, (RANK, RANK), 0)
    lane_all = lax.broadcasted_iota(jnp.int32, (RANK, RANK), 1)
    work[:, :RANK] = gram
    work[:, RANK:] = jnp.where(row_all == lane_all, 1.0, 0.0)
    count = PANEL // 8
    for start in range(0, RANK, PANEL):
        left = [work[start + 8 * v : start + 8 * v + 8, :RANK] for v in range(count)]
        right = [work[start + 8 * v : start + 8 * v + 8, RANK:] for v in range(count)]
        scale = [jnp.ones((8, RANK), f32) for _ in range(count)]
        for strip in range(0, PANEL, STRIP):
            column = {}
            for m in range(strip, strip + STRIP):
                for v in range(strip // 8, count):
                    column[m, v] = spread(left[v][:, start + m : start + m + 1])
            for i in range(strip, strip + STRIP):
                at, r = i // 8, i % 8
                pivot = spread(column[i, at][r : r + 1, :])
                inverse = 1.0 / pivot
                scale[at] = jnp.where(row == r, pivot, scale[at])
                later = range(i + 1, strip + STRIP)
                tops = {m: spread(column[m, at][r : r + 1, :]) for m in later}
                left_top, right_top = spread(left[at][r : r + 1, :]), spread(right[at][r : r + 1, :])
                for v in range(at, count):
                    if v == at and r == 7:
                        continue
                    ratio = column[i, v] * inverse
                    if v == at:
                        ratio = jnp.where(row > r, ratio, 0.0)
                    for m in later:
                        column[m, v] = column[m, v] - ratio * tops[m]
                    left[v] = left[v] - ratio * left_top
                    right[v] = right[v] - ratio * right_top
            between((start + strip) // STRIP)
        scale = [lax.rsqrt(v) for v in scale]
        upper = jnp.concatenate([v * w for v, w in zip(left, scale)], axis=0)
        both = jnp.concatenate([upper, jnp.concatenate([v * w for v, w in zip(right, scale)], axis=0)], axis=1)
        work[start : start + PANEL, :] = both
        below = start + PANEL
        if below < RANK:
            lane = lax.broadcasted_iota(jnp.int32, (PANEL, RANK), 1)
            update = dot_rows(jnp.where(lane >= below, upper, 0.0), both, HIGHEST)
            work[below:, :] = work[below:, :] - update[below:, :]
    return work[:, RANK:]


def kernel(
    momentum, gradient, factor, summed, left_basis, new_factor,
    grad, fac, s1, s2, s3, f12, f3, part, core_in, cross, a_full, grams, gram_all, gram_part, work, bt, rt, rsa, rsb,
    squares, right_rows,
    load_sem, a_send, a_recv, g_send, g_recv, r_send, r_recv,
):
    f, t = lax.axis_index("fsdp"), lax.axis_index("tensor")
    z, y = f // SIDE, lax.rem(f, SIDE)
    x, c = t // 2, lax.rem(t, 2)
    other_core = (f, x * 2 + 1 - c)
    x_peers = [(f, lax.rem(x + k, SIDE) * 2 + c) for k in range(1, SIDE)]
    far = lambda k: min(k, SIDE - k)
    hops = sorted(((j, k) for j in range(SIDE) for k in range(SIDE) if j + k), key=lambda v: (-far(v[0]) - far(v[1]), v))
    f_peers = [(lax.rem(z + j, SIDE) * SIDE + lax.rem(y + k, SIDE), t) for j, k in hops]
    hops = sorted(((j, k) for j in range(SIDE) for k in range(2) if j + k), key=lambda v: (-far(v[0]), v))
    t_peers = [(f, lax.rem(x + j, SIDE) * 2 + lax.rem(c + k, 2)) for j, k in hops]
    along = {
        "y": (y, [lax.rem(y + k, SIDE) for k in range(1, SIDE)], lambda v: (z * SIDE + v, t)),
        "z": (z, [lax.rem(z + k, SIDE) for k in range(1, SIDE)], lambda v: (v * SIDE + y, t)),
    }
    sent = []

    def remote(src, dst, send, recv, to):
        copy = pltpu.make_async_remote_copy(
            src_ref=src, dst_ref=dst, send_sem=send, recv_sem=recv, device_id=to, device_id_type=MESH
        )
        copy.start()
        sent.append(copy)
        return copy

    loads = [pltpu.make_async_copy(factor, fac, load_sem.at[2 * CHUNKS])]
    for i in range(CHUNKS):
        rows = pl.ds(i * CHUNK, CHUNK)
        loads.append(pltpu.make_async_copy(momentum.at[rows], summed.at[rows], load_sem.at[2 * i]))
        loads.append(pltpu.make_async_copy(gradient.at[rows], grad.at[rows], load_sem.at[2 * i + 1]))
    for load in loads:
        load.start()

    barrier = pltpu.get_barrier_semaphore()
    greeted = t_peers + f_peers
    for peer in greeted:
        pl.semaphore_signal(barrier, inc=1, device_id=peer, device_id_type=MESH)

    def add_and_split(i, at, width):
        where = (pl.ds(i * CHUNK, CHUNK), pl.ds(at, width))
        total = summed[where] + grad[where].astype(f32)
        summed[where] = total
        s1[where], s2[where], s3[where] = split3(total)

    def wait_rows(i):
        loads[1 + 2 * i].wait()
        loads[2 + 2 * i].wait()

    loads[0].wait()
    for at, width in tiles(COLS):
        here = pl.ds(at, width)
        f12[here, :RANK], f12[here, RANK:], f3[here, :] = split3(fac[here, :])
    wait_rows(0)
    for at, width in tiles(COLS):
        add_and_split(0, at, width)

    half = CHUNK // 2
    core_copies, cross_copies, back_copies = [], [], []

    def pass_across(i):
        core_copies[i].wait_recv()
        cross[i, x] = part[i, pl.ds(c * half, half)] + core_in[i]
        cross_copies.append(
            [
                remote(cross.at[i, x], cross.at[i, x], a_send.at[CHUNKS + 3 * i + k], a_recv.at[CHUNKS + 3 * i + k], peer)
                for k, peer in enumerate(x_peers)
            ]
        )

    def pass_back(i):
        for copy in cross_copies[i]:
            copy.wait_recv()
        mine = pl.ds(i * CHUNK + c * half, half)
        a_full[mine, :] = (cross[i, 0] + cross[i, 1]) + (cross[i, 2] + cross[i, 3])
        back_copies.append(
            remote(a_full.at[mine], a_full.at[mine], a_send.at[4 * CHUNKS + i], a_recv.at[4 * CHUNKS + i], other_core)
        )

    for i in range(CHUNKS):
        rows = pl.ds(i * CHUNK, CHUNK)
        if i + 1 < CHUNKS:
            wait_rows(i + 1)
        pair = jnp.zeros((CHUNK, 2 * RANK), f32)
        small = jnp.zeros((CHUNK, RANK), f32)
        for at, width in tiles(COLS):
            if i + 1 < CHUNKS:
                add_and_split(i + 1, at, width)
            here = pl.ds(at, width)
            pair = pair + (dot(s1[rows, here], f12[here, :]) + dot(s2[rows, here], f12[here, :]))
            small = small + (dot(s1[rows, here], f3[here, :]) + dot(s3[rows, here], f12[here, :RANK]))
        part[i] = pair[:, :RANK] + (pair[:, RANK:] + small)
        if i == 0:
            pl.semaphore_wait(barrier, len(greeted))
        core_copies.append(
            remote(part.at[i, pl.ds((1 - c) * half, half)], core_in.at[i], a_send.at[i], a_recv.at[i], other_core)
        )
        if i > 0:
            pass_across(i - 1)
    pass_across(CHUNKS - 1)
    for i in range(CHUNKS):
        pass_back(i)
    for copy in back_copies:
        copy.wait_recv()

    def gram_send(k, rows):
        gram_part[...] = dot_rows(rows, rows, HIGHEST)
        share = RANK // TENSOR
        grams[k, f] = gram_part[pl.ds(pl.multiple_of(t * share, share), share), :]
        return [
            remote(grams.at[k, f], grams.at[k, f], g_send.at[k, n], g_recv.at[k, n], peer) for n, peer in enumerate(f_peers)
        ]

    def gram_share(k, copies):
        for copy in copies:
            copy.wait_recv()
        total = grams[k, 0]
        for n in range(1, FSDP):
            total = total + grams[k, n]
        gram_all[k, t] = total
        return [
            remote(gram_all.at[k, t], gram_all.at[k, t], g_send.at[k, FSDP - 1 + n], g_recv.at[k, FSDP - 1 + n], peer)
            for n, peer in enumerate(t_peers)
        ]

    def gram_take(k, copies):
        for copy in copies:
            copy.wait_recv()
        return gram_all[k].reshape(RANK, RANK)

    a = a_full[...]
    at1, at2, at3 = split3(a.T)
    stack = jnp.concatenate([at1, at2, at3], axis=0)
    chunk_rows = RANK // SIDE
    piece_rows = chunk_rows // SIDE
    moves = {}

    def cols_of(g):
        return pl.ds(GROUPS[g][0], GROUPS[g][1])

    def place(g):
        own = pl.multiple_of(along[GROUPS[g][2]][0] * chunk_rows, chunk_rows)
        return own, pl.multiple_of(own + along[GROUPS[g][3]][0] * piece_rows, piece_rows)

    def multiply(g):
        start, size, _, _ = GROUPS[g]
        for at, width in tiles(size):
            cols = pl.ds(start + at, width)
            one = dot(stack, s1[:, cols])
            two = dot(stack[: 2 * RANK], s2[:, cols])
            three = dot(at1, s3[:, cols])
            low = one[2 * RANK :] + (two[RANK:] + three)
            bt[:, cols] = one[:RANK] + ((one[RANK : 2 * RANK] + two[:RANK]) + low)

    def first_send(g):
        _, peers, where = along[GROUPS[g][2]]
        cols = cols_of(g)
        moves[0, g] = [
            remote(
                bt.at[pl.ds(v * chunk_rows, chunk_rows), cols], rsa.at[k, :, cols], r_send.at[0, g, k], r_recv.at[0, g, k], where(v)
            )
            for k, v in enumerate(peers)
        ]

    def second_send(g):
        for copy in moves[0, g]:
            copy.wait_recv()
        own, _ = place(g)
        cols = cols_of(g)
        mine = pl.ds(own, chunk_rows)
        bt[mine, cols] = (bt[mine, cols] + rsa[0, :, cols]) + (rsa[1, :, cols] + rsa[2, :, cols])
        _, peers, where = along[GROUPS[g][3]]
        moves[1, g] = [
            remote(
                bt.at[pl.ds(own + v * piece_rows, piece_rows), cols],
                rsb.at[k, :, cols], r_send.at[1, g, k], r_recv.at[1, g, k], where(v),
            )
            for k, v in enumerate(peers)
        ]

    def third_send(g):
        for copy in moves[1, g]:
            copy.wait_recv()
        _, at = place(g)
        cols = cols_of(g)
        mine = pl.ds(at, piece_rows)
        rt[mine, cols] = (bt[mine, cols] + rsb[0, :, cols]) + (rsb[1, :, cols] + rsb[2, :, cols])
        _, peers, where = along[GROUPS[g][3]]
        moves[2, g] = [
            remote(rt.at[mine, cols], rt.at[mine, cols], r_send.at[2, g, k], r_recv.at[2, g, k], where(v))
            for k, v in enumerate(peers)
        ]

    def fourth_send(g):
        for copy in moves[2, g]:
            copy.wait_recv()
        own, _ = place(g)
        cols = cols_of(g)
        mine = pl.ds(own, chunk_rows)
        _, peers, where = along[GROUPS[g][2]]
        moves[3, g] = [
            remote(rt.at[mine, cols], rt.at[mine, cols], r_send.at[3, g, k], r_recv.at[3, g, k], where(v))
            for k, v in enumerate(peers)
        ]

    steps = {"m": multiply, "f": first_send, "s": second_send, "t": third_send, "q": fourth_send}
    state = {"rows0": a}

    def round_step(name, k, inside):
        if name == "gram":
            if k == 1:
                state["rows1"] = dot_lanes(a, state["inverse0"], HIGHEST)
            state["sent"] = gram_send(k, state["rows%d" % k])
        elif name == "share":
            state["sent"] = gram_share(k, state["sent"])
        elif name == "take":
            state["gram"] = gram_take(k, state["sent"])
        else:
            state["inverse%d" % k] = cholesky_inverse(work, state["gram"], inside)

    for word in " ".join(PLAN).split():
        word, _, hooks = word.partition(":")

        def inside(strip, hooks=hooks):
            for hook in hooks.split(","):
                when, _, step = hook.partition("=")
                if when == str(strip):
                    steps[step[0]](int(step[1]))

        if word[0] in steps and len(word) == 2:
            steps[word[0]](int(word[1]))
        else:
            round_step(word[:-1], int(word[-1]) - 1, inside)
    second_left, inverse_one, inverse_two = state["rows1"], state["inverse0"], state["inverse1"]
    turn = dot(inverse_two, inverse_one, HIGHEST)
    basis = dot_lanes(second_left, inverse_two, HIGHEST)
    left_basis[...] = basis
    q12 = jnp.concatenate(split2(basis * (1.0 - momentum_decay)), axis=1)
    t1, t2, t3 = split3(turn)
    t12 = jnp.concatenate([t1, t2], axis=1)
    t13 = jnp.concatenate([t1, t3], axis=1)
    energy = jnp.zeros((RANK, RANK), f32)
    for g, (start, size, _, _) in enumerate(GROUPS):
        for copy in moves[3, g]:
            copy.wait_recv()
        for at, width in tiles(size):
            cols = pl.ds(start + at, width)
            r1, r2, r3 = split3(rt[:, cols])
            right = dot(t12, jnp.concatenate([r1, r1], axis=0)) + (
                dot(t12, jnp.concatenate([r2, r2], axis=0)) + dot(t13, jnp.concatenate([r3, r1], axis=0))
            )
            right_rows[:, cols] = right
            for lane in range(0, width, RANK):
                tile = right[:, lane : lane + RANK]
                energy = energy + tile * tile
    squares[t] = dot_lanes(jnp.ones((8, RANK), f32), energy, HIGHEST)
    last = [
        remote(squares.at[t], squares.at[t], a_send.at[5 * CHUNKS + n], a_recv.at[5 * CHUNKS + n], peer)
        for n, peer in enumerate(t_peers)
    ]
    for n, (start, size, _, _) in enumerate(GROUPS):
        for at, width in tiles(size):
            cols = pl.ds(start + at, width)
            right = right_rows[:, cols]
            rounded = right.astype(bf16)
            summed[:, cols] = summed[:, cols] - dot(q12, jnp.concatenate([rounded, rounded], axis=0))
            new_factor[cols, :] = right.T
    for copy in last:
        copy.wait_recv()
    total = squares[0]
    for n in range(1, TENSOR):
        total = total + squares[n]
    new_factor[...] = new_factor[...] * lax.rsqrt(total[:1] + 1e-06)
    for copy in sent:
        copy.wait_send()


def write_out(*refs):
    sources, targets, sems = refs[:3], refs[3:6], refs[6]
    copies = [pltpu.make_async_copy(source, target, sems.at[k]) for k, (source, target) in enumerate(zip(sources, targets))]
    for copy in copies:
        copy.start()
    for copy in copies:
        copy.wait()


def per_device(momentum, gradient, factor):
    dma = pltpu.SemaphoreType.DMA
    results = pl.pallas_call(
        kernel,
        out_shape=(
            pltpu.VMEM((ROWS, COLS), f32),
            pltpu.VMEM((ROWS, RANK), f32),
            pltpu.VMEM((COLS, RANK), f32),
        ),
        in_specs=[pl.BlockSpec(memory_space=pltpu.HBM)] * 3,
        out_specs=[pl.BlockSpec(memory_space=pltpu.VMEM)] * 3,
        scratch_shapes=[
            pltpu.VMEM((ROWS, COLS), bf16),
            pltpu.VMEM((COLS, RANK), f32),
            pltpu.VMEM((ROWS, COLS), bf16),
            pltpu.VMEM((ROWS, COLS), bf16),
            pltpu.VMEM((ROWS, COLS), bf16),
            pltpu.VMEM((COLS, 2 * RANK), bf16),
            pltpu.VMEM((COLS, RANK), bf16),
            pltpu.VMEM((CHUNKS, CHUNK, RANK), f32),
            pltpu.VMEM((CHUNKS, CHUNK // 2, RANK), f32),
            pltpu.VMEM((CHUNKS, SIDE, CHUNK // 2, RANK), f32),
            pltpu.VMEM((ROWS, RANK), f32),
            pltpu.VMEM((2, FSDP, RANK // TENSOR, RANK), f32),
            pltpu.VMEM((2, TENSOR, RANK // TENSOR, RANK), f32),
            pltpu.VMEM((RANK, RANK), f32),
            pltpu.VMEM((RANK, 2 * RANK), f32),
            pltpu.VMEM((RANK, COLS), f32),
            pltpu.VMEM((RANK, COLS), f32),
            pltpu.VMEM((SIDE - 1, RANK // SIDE, COLS), f32),
            pltpu.VMEM((SIDE - 1, RANK // FSDP, COLS), f32),
            pltpu.VMEM((TENSOR, 8, RANK), f32),
            pltpu.VMEM((RANK, COLS), f32),
            dma((2 * CHUNKS + 1,)),
            dma((5 * CHUNKS + TENSOR - 1,)),
            dma((5 * CHUNKS + TENSOR - 1,)),
            dma((2, FSDP + TENSOR - 2)),
            dma((2, FSDP + TENSOR - 2)),
            dma((4, len(GROUPS), SIDE - 1)),
            dma((4, len(GROUPS), SIDE - 1)),
        ],
        compiler_params=pltpu.CompilerParams(collective_id=0, has_side_effects=True, vmem_limit_bytes=44 << 20),
        cost_estimate=pl.CostEstimate(flops=8 * 10**9, bytes_accessed=20 * 10**6, transcendentals=0),
        name="dion_update",
    )(*(pltpu.with_memory_space_constraint(v, pltpu.HBM) for v in (momentum, gradient, factor)))
    return pl.pallas_call(
        write_out,
        out_shape=tuple(jax.ShapeDtypeStruct(v.shape, v.dtype) for v in results),
        in_specs=[pl.BlockSpec(memory_space=pl.ANY)] * 3,
        out_specs=[pl.BlockSpec(memory_space=pl.ANY)] * 3,
        scratch_shapes=[dma((3,))],
        compiler_params=pltpu.CompilerParams(vmem_limit_bytes=1 << 20),
        cost_estimate=pl.CostEstimate(flops=0, bytes_accessed=9 * 10**6, transcendentals=0),
        name="write_out",
    )(*(pltpu.with_memory_space_constraint(v, pltpu.VMEM) for v in results))


def solution(mesh):
    return jax.shard_map(
        per_device,
        mesh=mesh,
        in_specs=(P("fsdp", "tensor"), P("fsdp", "tensor"), P("tensor", None)),
        out_specs=(P("fsdp", "tensor"), P("fsdp", None), P("tensor", None)),
        check_vma=False,
    )
```

```python
import jax
import jax.numpy as jnp
from jax import lax
from jax.experimental import pallas as pl
from jax.experimental.pallas import tpu as pltpu
from jax.sharding import PartitionSpec as P

MESH = pl.DeviceIdType.MESH
HIGHEST = lax.Precision.HIGHEST
f32, bf16 = jnp.float32, jnp.bfloat16
momentum_decay = 0.9

ROWS, COLS, RANK = 512, 3328, 128
FSDP, TENSOR, SIDE = 16, 8, 4
CHUNKS = 4
CHUNK = ROWS // CHUNKS
GROUPS = ((0, 896, "y", "z"), (896, 896, "z", "y"), (1792, 768, "y", "z"), (2560, 768, "z", "y"))
WIDE = 256
PANEL, STRIP = 64, 16
PIECES = (8, 1, 2)
PLAN = (
    "gram1 m0 f0 m1", "f1 m2 m3 share1", "f2 f3 take1", "chol1:0=s0,0=s1,7=s2,7=s3", "gram2 t0 t1 t2", "t3 q0 q1 share2",
    "q2 q3 take2 chol2",
)


def dot(left, right, precision=None):
    return jnp.dot(left, right, precision=precision, preferred_element_type=f32)


def dot_rows(left, right, precision=None):
    return lax.dot_general(left, right, (((0,), (0,)), ((), ())), precision=precision, preferred_element_type=f32)


def dot_lanes(left, right, precision=None):
    return lax.dot_general(left, right, (((1,), (1,)), ((), ())), precision=precision, preferred_element_type=f32)


def split3(x):
    first = x.astype(bf16)
    rest = x - first.astype(f32)
    second = rest.astype(bf16)
    third = (rest - second.astype(f32)).astype(bf16)
    return first, second, third


def split2(x):
    first = x.astype(bf16)
    return first, (x - first.astype(f32)).astype(bf16)


def tiles(width, step=WIDE):
    return [(at, min(step, width - at)) for at in range(0, width, step)]


def cholesky_inverse(work, gram, between):
    row = lax.broadcasted_iota(jnp.int32, (8, RANK), 0)
    spread = lambda x: jnp.broadcast_to(x, (8, RANK))
    row_all = lax.broadcasted_iota(jnp.int32, (RANK, RANK), 0)
    lane_all = lax.broadcasted_iota(jnp.int32, (RANK, RANK), 1)
    work[:, :RANK] = gram
    work[:, RANK:] = jnp.where(row_all == lane_all, 1.0, 0.0)
    count = PANEL // 8
    for start in range(0, RANK, PANEL):
        left = [work[start + 8 * v : start + 8 * v + 8, :RANK] for v in range(count)]
        right = [work[start + 8 * v : start + 8 * v + 8, RANK:] for v in range(count)]
        scale = [jnp.ones((8, RANK), f32) for _ in range(count)]
        for strip in range(0, PANEL, STRIP):
            column = {}
            for m in range(strip, strip + STRIP):
                for v in range(strip // 8, count):
                    column[m, v] = spread(left[v][:, start + m : start + m + 1])
            for i in range(strip, strip + STRIP):
                at, r = i // 8, i % 8
                pivot = spread(column[i, at][r : r + 1, :])
                inverse = 1.0 / pivot
                scale[at] = jnp.where(row == r, pivot, scale[at])
                later = range(i + 1, strip + STRIP)
                tops = {m: spread(column[m, at][r : r + 1, :]) for m in later}
                left_top, right_top = spread(left[at][r : r + 1, :]), spread(right[at][r : r + 1, :])
                for v in range(at, count):
                    if v == at and r == 7:
                        continue
                    ratio = column[i, v] * inverse
                    if v == at:
                        ratio = jnp.where(row > r, ratio, 0.0)
                    for m in later:
                        column[m, v] = column[m, v] - ratio * tops[m]
                    left[v] = left[v] - ratio * left_top
                    right[v] = right[v] - ratio * right_top
            between((start + strip) // STRIP)
        scale = [lax.rsqrt(v) for v in scale]
        upper = jnp.concatenate([v * w for v, w in zip(left, scale)], axis=0)
        both = jnp.concatenate([upper, jnp.concatenate([v * w for v, w in zip(right, scale)], axis=0)], axis=1)
        work[start : start + PANEL, :] = both
        below = start + PANEL
        if below < RANK:
            lane = lax.broadcasted_iota(jnp.int32, (PANEL, RANK), 1)
            update = dot_rows(jnp.where(lane >= below, upper, 0.0), both, HIGHEST)
            work[below:, :] = work[below:, :] - update[below:, :]
    return work[:, RANK:]


def kernel(
    momentum, gradient, factor, summed, left_basis, new_factor,
    grad, fac, s1, s2, s3, f12, f3, part, core_in, cross, a_full, grams, gram_all, gram_part, work, bt, rt, rsa, rsb,
    squares, right_rows,
    load_sem, a_send, a_recv, g_send, g_recv, r_send, r_recv,
):
    f, t = lax.axis_index("fsdp"), lax.axis_index("tensor")
    z, y = f // SIDE, lax.rem(f, SIDE)
    x, c = t // 2, lax.rem(t, 2)
    other_core = (f, x * 2 + 1 - c)
    x_peers = [(f, lax.rem(x + k, SIDE) * 2 + c) for k in range(1, SIDE)]
    far = lambda k: min(k, SIDE - k)
    hops = sorted(((j, k) for j in range(SIDE) for k in range(SIDE) if j + k), key=lambda v: (-far(v[0]) - far(v[1]), v))
    f_peers = [(lax.rem(z + j, SIDE) * SIDE + lax.rem(y + k, SIDE), t) for j, k in hops]
    hops = sorted(((j, k) for j in range(SIDE) for k in range(2) if j + k), key=lambda v: (-far(v[0]), v))
    t_peers = [(f, lax.rem(x + j, SIDE) * 2 + lax.rem(c + k, 2)) for j, k in hops]
    along = {
        "y": (y, [lax.rem(y + k, SIDE) for k in range(1, SIDE)], lambda v: (z * SIDE + v, t)),
        "z": (z, [lax.rem(z + k, SIDE) for k in range(1, SIDE)], lambda v: (v * SIDE + y, t)),
    }
    sent = []

    def remote(src, dst, send, recv, to):
        copy = pltpu.make_async_remote_copy(
            src_ref=src, dst_ref=dst, send_sem=send, recv_sem=recv, device_id=to, device_id_type=MESH
        )
        copy.start()
        sent.append(copy)
        return copy

    loads = [pltpu.make_async_copy(factor, fac, load_sem.at[2 * CHUNKS])]
    for i in range(CHUNKS):
        rows = pl.ds(i * CHUNK, CHUNK)
        loads.append(pltpu.make_async_copy(momentum.at[rows], summed.at[rows], load_sem.at[2 * i]))
        loads.append(pltpu.make_async_copy(gradient.at[rows], grad.at[rows], load_sem.at[2 * i + 1]))
    for load in loads:
        load.start()

    barrier = pltpu.get_barrier_semaphore()
    greeted = t_peers + f_peers
    for peer in greeted:
        pl.semaphore_signal(barrier, inc=1, device_id=peer, device_id_type=MESH)

    def add_and_split(i, at, width):
        where = (pl.ds(i * CHUNK, CHUNK), pl.ds(at, width))
        total = summed[where] + grad[where].astype(f32)
        summed[where] = total
        s1[where], s2[where], s3[where] = split3(total)

    def wait_rows(i):
        loads[1 + 2 * i].wait()
        loads[2 + 2 * i].wait()

    loads[0].wait()
    for at, width in tiles(COLS):
        here = pl.ds(at, width)
        f12[here, :RANK], f12[here, RANK:], f3[here, :] = split3(fac[here, :])
    wait_rows(0)
    for at, width in tiles(COLS):
        add_and_split(0, at, width)

    half = CHUNK // 2
    core_copies, cross_copies, back_copies = [], [], []

    def pass_across(i):
        core_copies[i].wait_recv()
        cross[i, x] = part[i, pl.ds(c * half, half)] + core_in[i]
        cross_copies.append(
            [
                remote(cross.at[i, x], cross.at[i, x], a_send.at[CHUNKS + 3 * i + k], a_recv.at[CHUNKS + 3 * i + k], peer)
                for k, peer in enumerate(x_peers)
            ]
        )

    def pass_back(i):
        for copy in cross_copies[i]:
            copy.wait_recv()
        mine = pl.ds(i * CHUNK + c * half, half)
        a_full[mine, :] = (cross[i, 0] + cross[i, 1]) + (cross[i, 2] + cross[i, 3])
        back_copies.append(
            remote(a_full.at[mine], a_full.at[mine], a_send.at[4 * CHUNKS + i], a_recv.at[4 * CHUNKS + i], other_core)
        )

    for i in range(CHUNKS):
        rows = pl.ds(i * CHUNK, CHUNK)
        if i + 1 < CHUNKS:
            wait_rows(i + 1)
        pair = jnp.zeros((CHUNK, 2 * RANK), f32)
        small = jnp.zeros((CHUNK, RANK), f32)
        for at, width in tiles(COLS):
            if i + 1 < CHUNKS:
                add_and_split(i + 1, at, width)
            here = pl.ds(at, width)
            pair = pair + (dot(s1[rows, here], f12[here, :]) + dot(s2[rows, here], f12[here, :]))
            small = small + (dot(s1[rows, here], f3[here, :]) + dot(s3[rows, here], f12[here, :RANK]))
        part[i] = pair[:, :RANK] + (pair[:, RANK:] + small)
        if i == 0:
            pl.semaphore_wait(barrier, len(greeted))
        core_copies.append(
            remote(part.at[i, pl.ds((1 - c) * half, half)], core_in.at[i], a_send.at[i], a_recv.at[i], other_core)
        )
        if i > 0:
            pass_across(i - 1)
    pass_across(CHUNKS - 1)
    for i in range(CHUNKS):
        pass_back(i)
    for copy in back_copies:
        copy.wait_recv()

    def gram_send(k, rows):
        gram_part[...] = dot_rows(rows, rows, HIGHEST)
        share = RANK // TENSOR
        grams[k, f] = gram_part[pl.ds(pl.multiple_of(t * share, share), share), :]
        return [
            remote(grams.at[k, f], grams.at[k, f], g_send.at[k, n], g_recv.at[k, n], peer) for n, peer in enumerate(f_peers)
        ]

    def gram_share(k, copies):
        for copy in copies:
            copy.wait_recv()
        total = grams[k, 0]
        for n in range(1, FSDP):
            total = total + grams[k, n]
        gram_all[k, t] = total
        return [
            remote(gram_all.at[k, t], gram_all.at[k, t], g_send.at[k, FSDP - 1 + n], g_recv.at[k, FSDP - 1 + n], peer)
            for n, peer in enumerate(t_peers)
        ]

    def gram_take(k, copies):
        for copy in copies:
            copy.wait_recv()
        return gram_all[k].reshape(RANK, RANK)

    a = a_full[...]
    at1, at2, at3 = split3(a.T)
    stack = jnp.concatenate([at1, at2, at3], axis=0)
    chunk_rows = RANK // SIDE
    piece_rows = chunk_rows // SIDE
    moves = {}

    def cols_of(g):
        return pl.ds(GROUPS[g][0], GROUPS[g][1])

    def place(g):
        own = pl.multiple_of(along[GROUPS[g][2]][0] * chunk_rows, chunk_rows)
        return own, pl.multiple_of(own + along[GROUPS[g][3]][0] * piece_rows, piece_rows)

    def multiply(g):
        start, size, _, _ = GROUPS[g]
        for at, width in tiles(size):
            cols = pl.ds(start + at, width)
            one = dot(stack, s1[:, cols])
            two = dot(stack[: 2 * RANK], s2[:, cols])
            three = dot(at1, s3[:, cols])
            low = one[2 * RANK :] + (two[RANK:] + three)
            bt[:, cols] = one[:RANK] + ((one[RANK : 2 * RANK] + two[:RANK]) + low)

    def first_send(g):
        _, peers, where = along[GROUPS[g][2]]
        cols = cols_of(g)
        moves[0, g] = [
            remote(
                bt.at[pl.ds(v * chunk_rows, chunk_rows), cols], rsa.at[k, :, cols], r_send.at[0, g, k], r_recv.at[0, g, k], where(v)
            )
            for k, v in enumerate(peers)
        ]

    def second_send(g):
        for copy in moves[0, g]:
            copy.wait_recv()
        own, _ = place(g)
        cols = cols_of(g)
        mine = pl.ds(own, chunk_rows)
        bt[mine, cols] = (bt[mine, cols] + rsa[0, :, cols]) + (rsa[1, :, cols] + rsa[2, :, cols])
        _, peers, where = along[GROUPS[g][3]]
        moves[1, g] = [
            remote(
                bt.at[pl.ds(own + v * piece_rows, piece_rows), cols],
                rsb.at[k, :, cols], r_send.at[1, g, k], r_recv.at[1, g, k], where(v),
            )
            for k, v in enumerate(peers)
        ]

    def third_send(g):
        for copy in moves[1, g]:
            copy.wait_recv()
        _, at = place(g)
        cols = cols_of(g)
        mine = pl.ds(at, piece_rows)
        rt[mine, cols] = (bt[mine, cols] + rsb[0, :, cols]) + (rsb[1, :, cols] + rsb[2, :, cols])
        _, peers, where = along[GROUPS[g][3]]
        moves[2, g] = [
            remote(rt.at[mine, cols], rt.at[mine, cols], r_send.at[2, g, k], r_recv.at[2, g, k], where(v))
            for k, v in enumerate(peers)
        ]

    def fourth_send(g):
        for copy in moves[2, g]:
            copy.wait_recv()
        own, _ = place(g)
        cols = cols_of(g)
        mine = pl.ds(own, chunk_rows)
        _, peers, where = along[GROUPS[g][2]]
        moves[3, g] = [
            remote(rt.at[mine, cols], rt.at[mine, cols], r_send.at[3, g, k], r_recv.at[3, g, k], where(v))
            for k, v in enumerate(peers)
        ]

    steps = {"m": multiply, "f": first_send, "s": second_send, "t": third_send, "q": fourth_send}
    state = {"rows0": a}

    def round_step(name, k, inside):
        if name == "gram":
            if k == 1:
                state["rows1"] = dot_lanes(a, state["inverse0"], HIGHEST)
            state["sent"] = gram_send(k, state["rows%d" % k])
        elif name == "share":
            state["sent"] = gram_share(k, state["sent"])
        elif name == "take":
            state["gram"] = gram_take(k, state["sent"])
        else:
            state["inverse%d" % k] = cholesky_inverse(work, state["gram"], inside)

    for word in " ".join(PLAN).split():
        word, _, hooks = word.partition(":")

        def inside(strip, hooks=hooks):
            for hook in hooks.split(","):
                when, _, step = hook.partition("=")
                if when == str(strip):
                    steps[step[0]](int(step[1]))

        if word[0] in steps and len(word) == 2:
            steps[word[0]](int(word[1]))
        else:
            round_step(word[:-1], int(word[-1]) - 1, inside)
    second_left, inverse_one, inverse_two = state["rows1"], state["inverse0"], state["inverse1"]
    turn = dot(inverse_two, inverse_one, HIGHEST)
    basis = dot_lanes(second_left, inverse_two, HIGHEST)
    left_basis[...] = basis
    q12 = jnp.concatenate(split2(basis * (1.0 - momentum_decay)), axis=1)
    t1, t2, t3 = split3(turn)
    t12 = jnp.concatenate([t1, t2], axis=1)
    t13 = jnp.concatenate([t1, t3], axis=1)
    energy = jnp.zeros((RANK, RANK), f32)
    for g, (start, size, _, _) in enumerate(GROUPS):
        for copy in moves[3, g]:
            copy.wait_recv()
        for at, width in tiles(size):
            cols = pl.ds(start + at, width)
            r1, r2, r3 = split3(rt[:, cols])
            right = dot(t12, jnp.concatenate([r1, r1], axis=0)) + (
                dot(t12, jnp.concatenate([r2, r2], axis=0)) + dot(t13, jnp.concatenate([r3, r1], axis=0))
            )
            right_rows[:, cols] = right
            for lane in range(0, width, RANK):
                tile = right[:, lane : lane + RANK]
                energy = energy + tile * tile
    squares[t] = dot_lanes(jnp.ones((8, RANK), f32), energy, HIGHEST)
    last = [
        remote(squares.at[t], squares.at[t], a_send.at[5 * CHUNKS + n], a_recv.at[5 * CHUNKS + n], peer)
        for n, peer in enumerate(t_peers)
    ]
    for n, (start, size, _, _) in enumerate(GROUPS):
        for at, width in tiles(size):
            cols = pl.ds(start + at, width)
            right = right_rows[:, cols]
            rounded = right.astype(bf16)
            summed[:, cols] = summed[:, cols] - dot(q12, jnp.concatenate([rounded, rounded], axis=0))
            new_factor[cols, :] = right.T
    for copy in last:
        copy.wait_recv()
    total = squares[0]
    for n in range(1, TENSOR):
        total = total + squares[n]
    new_factor[...] = new_factor[...] * lax.rsqrt(total[:1] + 1e-06)
    for copy in sent:
        copy.wait_send()


def write_out(*refs):
    copies = []
    for source, target, pieces in zip(refs[:3], refs[3:6], PIECES):
        size = source.shape[0] // pieces
        for k in range(pieces):
            rows = pl.ds(k * size, size)
            copies.append(pltpu.make_async_copy(source.at[rows], target.at[rows], refs[6].at[len(copies)]))
            copies[-1].start()
    for copy in copies:
        copy.wait()


def per_device(momentum, gradient, factor):
    dma = pltpu.SemaphoreType.DMA
    results = pl.pallas_call(
        kernel,
        out_shape=(
            pltpu.VMEM((ROWS, COLS), f32),
            pltpu.VMEM((ROWS, RANK), f32),
            pltpu.VMEM((COLS, RANK), f32),
        ),
        in_specs=[pl.BlockSpec(memory_space=pltpu.HBM)] * 3,
        out_specs=[pl.BlockSpec(memory_space=pltpu.VMEM)] * 3,
        scratch_shapes=[
            pltpu.VMEM((ROWS, COLS), bf16),
            pltpu.VMEM((COLS, RANK), f32),
            pltpu.VMEM((ROWS, COLS), bf16),
            pltpu.VMEM((ROWS, COLS), bf16),
            pltpu.VMEM((ROWS, COLS), bf16),
            pltpu.VMEM((COLS, 2 * RANK), bf16),
            pltpu.VMEM((COLS, RANK), bf16),
            pltpu.VMEM((CHUNKS, CHUNK, RANK), f32),
            pltpu.VMEM((CHUNKS, CHUNK // 2, RANK), f32),
            pltpu.VMEM((CHUNKS, SIDE, CHUNK // 2, RANK), f32),
            pltpu.VMEM((ROWS, RANK), f32),
            pltpu.VMEM((2, FSDP, RANK // TENSOR, RANK), f32),
            pltpu.VMEM((2, TENSOR, RANK // TENSOR, RANK), f32),
            pltpu.VMEM((RANK, RANK), f32),
            pltpu.VMEM((RANK, 2 * RANK), f32),
            pltpu.VMEM((RANK, COLS), f32),
            pltpu.VMEM((RANK, COLS), f32),
            pltpu.VMEM((SIDE - 1, RANK // SIDE, COLS), f32),
            pltpu.VMEM((SIDE - 1, RANK // FSDP, COLS), f32),
            pltpu.VMEM((TENSOR, 8, RANK), f32),
            pltpu.VMEM((RANK, COLS), f32),
            dma((2 * CHUNKS + 1,)),
            dma((5 * CHUNKS + TENSOR - 1,)),
            dma((5 * CHUNKS + TENSOR - 1,)),
            dma((2, FSDP + TENSOR - 2)),
            dma((2, FSDP + TENSOR - 2)),
            dma((4, len(GROUPS), SIDE - 1)),
            dma((4, len(GROUPS), SIDE - 1)),
        ],
        compiler_params=pltpu.CompilerParams(collective_id=0, has_side_effects=True, vmem_limit_bytes=44 << 20),
        cost_estimate=pl.CostEstimate(flops=8 * 10**9, bytes_accessed=20 * 10**6, transcendentals=0),
        name="dion_update",
    )(*(pltpu.with_memory_space_constraint(v, pltpu.HBM) for v in (momentum, gradient, factor)))
    return pl.pallas_call(
        write_out,
        out_shape=tuple(jax.ShapeDtypeStruct(v.shape, v.dtype) for v in results),
        in_specs=[pl.BlockSpec(memory_space=pl.ANY)] * 3,
        out_specs=[pl.BlockSpec(memory_space=pl.ANY)] * 3,
        scratch_shapes=[dma((sum(PIECES),))],
        compiler_params=pltpu.CompilerParams(vmem_limit_bytes=1 << 20),
        cost_estimate=pl.CostEstimate(flops=0, bytes_accessed=9 * 10**6, transcendentals=0),
        name="write_out",
    )(*(pltpu.with_memory_space_constraint(v, pltpu.VMEM) for v in results))


def solution(mesh):
    return jax.shard_map(
        per_device,
        mesh=mesh,
        in_specs=(P("fsdp", "tensor"), P("fsdp", "tensor"), P("tensor", None)),
        out_specs=(P("fsdp", "tensor"), P("fsdp", None), P("tensor", None)),
        check_vma=False,
    )
```

```python
import jax
import jax.numpy as jnp
from jax import lax
from jax.experimental import pallas as pl
from jax.experimental.pallas import tpu as pltpu
from jax.sharding import PartitionSpec as P

MESH = pl.DeviceIdType.MESH
HIGHEST = lax.Precision.HIGHEST
f32, bf16 = jnp.float32, jnp.bfloat16
momentum_decay = 0.9

ROWS, COLS, RANK = 512, 3328, 128
FSDP, TENSOR, SIDE = 16, 8, 4
CHUNKS = 4
CHUNK = ROWS // CHUNKS
GROUPS = ((0, 896, "y", "z"), (896, 896, "z", "y"), (1792, 768, "y", "z"), (2560, 768, "z", "y"))
WIDE = 256
PANEL, STRIP = 64, 16
PIECES = (8, 1, 2)
PLAN = (
    "gram1 m0 f0 m1", "f1 m2 m3 share1", "f2 f3 take1", "chol1:0=s0,0=s1,7=s2,7=s3", "gram2 t0 t1 t2", "t3 q0 q1 share2",
    "q2 q3 take2 chol2",
)


def dot(left, right, precision=None):
    return jnp.dot(left, right, precision=precision, preferred_element_type=f32)


def dot_rows(left, right, precision=None):
    return lax.dot_general(left, right, (((0,), (0,)), ((), ())), precision=precision, preferred_element_type=f32)


def dot_lanes(left, right, precision=None):
    return lax.dot_general(left, right, (((1,), (1,)), ((), ())), precision=precision, preferred_element_type=f32)


def split3(x):
    first = x.astype(bf16)
    rest = x - first.astype(f32)
    second = rest.astype(bf16)
    third = (rest - second.astype(f32)).astype(bf16)
    return first, second, third


def split2(x):
    first = x.astype(bf16)
    return first, (x - first.astype(f32)).astype(bf16)


def tiles(width, step=WIDE):
    return [(at, min(step, width - at)) for at in range(0, width, step)]


def cholesky_inverse(work, gram, between):
    row = lax.broadcasted_iota(jnp.int32, (8, RANK), 0)
    spread = lambda x: jnp.broadcast_to(x, (8, RANK))
    row_all = lax.broadcasted_iota(jnp.int32, (RANK, RANK), 0)
    lane_all = lax.broadcasted_iota(jnp.int32, (RANK, RANK), 1)
    work[:, :RANK] = gram
    work[:, RANK:] = jnp.where(row_all == lane_all, 1.0, 0.0)
    count = PANEL // 8
    for start in range(0, RANK, PANEL):
        left = [work[start + 8 * v : start + 8 * v + 8, :RANK] for v in range(count)]
        right = [work[start + 8 * v : start + 8 * v + 8, RANK:] for v in range(count)]
        scale = [jnp.ones((8, RANK), f32) for _ in range(count)]
        for strip in range(0, PANEL, STRIP):
            column = {}
            for m in range(strip, strip + STRIP):
                for v in range(strip // 8, count):
                    column[m, v] = spread(left[v][:, start + m : start + m + 1])
            for i in range(strip, strip + STRIP):
                at, r = i // 8, i % 8
                pivot = spread(column[i, at][r : r + 1, :])
                inverse = 1.0 / pivot
                scale[at] = jnp.where(row == r, pivot, scale[at])
                later = range(i + 1, strip + STRIP)
                tops = {m: spread(column[m, at][r : r + 1, :]) for m in later}
                left_top, right_top = spread(left[at][r : r + 1, :]), spread(right[at][r : r + 1, :])
                for v in range(at, count):
                    if v == at and r == 7:
                        continue
                    ratio = column[i, v] * inverse
                    if v == at:
                        ratio = jnp.where(row > r, ratio, 0.0)
                    for m in later:
                        column[m, v] = column[m, v] - ratio * tops[m]
                    left[v] = left[v] - ratio * left_top
                    right[v] = right[v] - ratio * right_top
            between((start + strip) // STRIP)
        scale = [lax.rsqrt(v) for v in scale]
        upper = jnp.concatenate([v * w for v, w in zip(left, scale)], axis=0)
        both = jnp.concatenate([upper, jnp.concatenate([v * w for v, w in zip(right, scale)], axis=0)], axis=1)
        work[start : start + PANEL, :] = both
        below = start + PANEL
        if below < RANK:
            lane = lax.broadcasted_iota(jnp.int32, (PANEL, RANK), 1)
            update = dot_rows(jnp.where(lane >= below, upper, 0.0), both, HIGHEST)
            work[below:, :] = work[below:, :] - update[below:, :]
    return work[:, RANK:]


def kernel(
    momentum, gradient, factor, summed, left_basis, new_factor,
    grad, fac, s1, s2, s3, f12, f3, part, core_in, cross, a_full, grams, gram_all, gram_part, work, bt, rt, rsa, rsb,
    squares, right_rows,
    load_sem, a_send, a_recv, g_send, g_recv, r_send, r_recv,
):
    f, t = lax.axis_index("fsdp"), lax.axis_index("tensor")
    z, y = f // SIDE, lax.rem(f, SIDE)
    x, c = t // 2, lax.rem(t, 2)
    other_core = (f, x * 2 + 1 - c)
    x_peers = [(f, lax.rem(x + k, SIDE) * 2 + c) for k in range(1, SIDE)]
    far = lambda k: min(k, SIDE - k)
    hops = sorted(((j, k) for j in range(SIDE) for k in range(SIDE) if j + k), key=lambda v: (-far(v[0]) - far(v[1]), v))
    f_peers = [(lax.rem(z + j, SIDE) * SIDE + lax.rem(y + k, SIDE), t) for j, k in hops]
    hops = sorted(((j, k) for j in range(SIDE) for k in range(2) if j + k), key=lambda v: (-far(v[0]), v))
    t_peers = [(f, lax.rem(x + j, SIDE) * 2 + lax.rem(c + k, 2)) for j, k in hops]
    along = {
        "y": (y, [lax.rem(y + k, SIDE) for k in range(1, SIDE)], lambda v: (z * SIDE + v, t)),
        "z": (z, [lax.rem(z + k, SIDE) for k in range(1, SIDE)], lambda v: (v * SIDE + y, t)),
    }
    sent = []

    def remote(src, dst, send, recv, to):
        copy = pltpu.make_async_remote_copy(
            src_ref=src, dst_ref=dst, send_sem=send, recv_sem=recv, device_id=to, device_id_type=MESH
        )
        copy.start()
        sent.append(copy)
        return copy

    loads = [pltpu.make_async_copy(factor, fac, load_sem.at[2 * CHUNKS])]
    for i in range(CHUNKS):
        rows = pl.ds(i * CHUNK, CHUNK)
        loads.append(pltpu.make_async_copy(momentum.at[rows], summed.at[rows], load_sem.at[2 * i]))
        loads.append(pltpu.make_async_copy(gradient.at[rows], grad.at[rows], load_sem.at[2 * i + 1]))
    for load in loads:
        load.start()

    barrier = pltpu.get_barrier_semaphore()
    greeted = t_peers + f_peers
    for peer in greeted:
        pl.semaphore_signal(barrier, inc=1, device_id=peer, device_id_type=MESH)

    def add_and_split(i, at, width):
        where = (pl.ds(i * CHUNK, CHUNK), pl.ds(at, width))
        total = summed[where] + grad[where].astype(f32)
        summed[where] = total
        s1[where], s2[where], s3[where] = split3(total)

    def wait_rows(i):
        loads[1 + 2 * i].wait()
        loads[2 + 2 * i].wait()

    loads[0].wait()
    for at, width in tiles(COLS):
        here = pl.ds(at, width)
        f12[here, :RANK], f12[here, RANK:], f3[here, :] = split3(fac[here, :])
    wait_rows(0)
    for at, width in tiles(COLS):
        add_and_split(0, at, width)

    half = CHUNK // 2
    core_copies, cross_copies, back_copies = [], [], []

    def pass_across(i):
        core_copies[i].wait_recv()
        cross[i, x] = part[i, pl.ds(c * half, half)] + core_in[i]
        cross_copies.append(
            [
                remote(cross.at[i, x], cross.at[i, x], a_send.at[CHUNKS + 3 * i + k], a_recv.at[CHUNKS + 3 * i + k], peer)
                for k, peer in enumerate(x_peers)
            ]
        )

    def pass_back(i):
        for copy in cross_copies[i]:
            copy.wait_recv()
        mine = pl.ds(i * CHUNK + c * half, half)
        a_full[mine, :] = (cross[i, 0] + cross[i, 1]) + (cross[i, 2] + cross[i, 3])
        back_copies.append(
            remote(a_full.at[mine], a_full.at[mine], a_send.at[4 * CHUNKS + i], a_recv.at[4 * CHUNKS + i], other_core)
        )

    for i in range(CHUNKS):
        rows = pl.ds(i * CHUNK, CHUNK)
        if i + 1 < CHUNKS:
            wait_rows(i + 1)
        pair = jnp.zeros((CHUNK, 2 * RANK), f32)
        small = jnp.zeros((CHUNK, RANK), f32)
        for at, width in tiles(COLS):
            if i + 1 < CHUNKS:
                add_and_split(i + 1, at, width)
            here = pl.ds(at, width)
            pair = pair + (dot(s1[rows, here], f12[here, :]) + dot(s2[rows, here], f12[here, :]))
            small = small + (dot(s1[rows, here], f3[here, :]) + dot(s3[rows, here], f12[here, :RANK]))
        part[i] = pair[:, :RANK] + (pair[:, RANK:] + small)
        if i == 0:
            pl.semaphore_wait(barrier, len(greeted))
        core_copies.append(
            remote(part.at[i, pl.ds((1 - c) * half, half)], core_in.at[i], a_send.at[i], a_recv.at[i], other_core)
        )
        if i > 0:
            pass_across(i - 1)
    pass_across(CHUNKS - 1)
    for i in range(CHUNKS):
        pass_back(i)
    for copy in back_copies:
        copy.wait_recv()

    def gram_send(k, rows):
        gram_part[...] = dot_rows(rows, rows, HIGHEST)
        share = RANK // TENSOR
        grams[k, f] = gram_part[pl.ds(pl.multiple_of(t * share, share), share), :]
        return [
            remote(grams.at[k, f], grams.at[k, f], g_send.at[k, n], g_recv.at[k, n], peer) for n, peer in enumerate(f_peers)
        ]

    def gram_share(k, copies):
        for copy in copies:
            copy.wait_recv()
        total = grams[k, 0]
        for n in range(1, FSDP):
            total = total + grams[k, n]
        gram_all[k, t] = total
        return [
            remote(gram_all.at[k, t], gram_all.at[k, t], g_send.at[k, FSDP - 1 + n], g_recv.at[k, FSDP - 1 + n], peer)
            for n, peer in enumerate(t_peers)
        ]

    def gram_take(k, copies):
        for copy in copies:
            copy.wait_recv()
        return gram_all[k].reshape(RANK, RANK)

    a = a_full[...]
    at1, at2, at3 = split3(a.T)
    stack = jnp.concatenate([at1, at2, at3], axis=0)
    chunk_rows = RANK // SIDE
    piece_rows = chunk_rows // SIDE
    moves = {}

    def cols_of(g):
        return pl.ds(GROUPS[g][0], GROUPS[g][1])

    def place(g):
        own = pl.multiple_of(along[GROUPS[g][2]][0] * chunk_rows, chunk_rows)
        return own, pl.multiple_of(own + along[GROUPS[g][3]][0] * piece_rows, piece_rows)

    def multiply(g):
        start, size, _, _ = GROUPS[g]
        for at, width in tiles(size):
            cols = pl.ds(start + at, width)
            one = dot(stack, s1[:, cols])
            two = dot(stack[: 2 * RANK], s2[:, cols])
            three = dot(at1, s3[:, cols])
            low = one[2 * RANK :] + (two[RANK:] + three)
            bt[:, cols] = one[:RANK] + ((one[RANK : 2 * RANK] + two[:RANK]) + low)

    def first_send(g):
        _, peers, where = along[GROUPS[g][2]]
        cols = cols_of(g)
        moves[0, g] = [
            remote(
                bt.at[pl.ds(v * chunk_rows, chunk_rows), cols], rsa.at[k, :, cols], r_send.at[0, g, k], r_recv.at[0, g, k], where(v)
            )
            for k, v in enumerate(peers)
        ]

    def second_send(g):
        for copy in moves[0, g]:
            copy.wait_recv()
        own, _ = place(g)
        cols = cols_of(g)
        mine = pl.ds(own, chunk_rows)
        bt[mine, cols] = (bt[mine, cols] + rsa[0, :, cols]) + (rsa[1, :, cols] + rsa[2, :, cols])
        _, peers, where = along[GROUPS[g][3]]
        moves[1, g] = [
            remote(
                bt.at[pl.ds(own + v * piece_rows, piece_rows), cols],
                rsb.at[k, :, cols], r_send.at[1, g, k], r_recv.at[1, g, k], where(v),
            )
            for k, v in enumerate(peers)
        ]

    def third_send(g):
        for copy in moves[1, g]:
            copy.wait_recv()
        _, at = place(g)
        cols = cols_of(g)
        mine = pl.ds(at, piece_rows)
        rt[mine, cols] = (bt[mine, cols] + rsb[0, :, cols]) + (rsb[1, :, cols] + rsb[2, :, cols])
        _, peers, where = along[GROUPS[g][3]]
        moves[2, g] = [
            remote(rt.at[mine, cols], rt.at[mine, cols], r_send.at[2, g, k], r_recv.at[2, g, k], where(v))
            for k, v in enumerate(peers)
        ]

    def fourth_send(g):
        for copy in moves[2, g]:
            copy.wait_recv()
        own, _ = place(g)
        cols = cols_of(g)
        mine = pl.ds(own, chunk_rows)
        _, peers, where = along[GROUPS[g][2]]
        moves[3, g] = [
            remote(rt.at[mine, cols], rt.at[mine, cols], r_send.at[3, g, k], r_recv.at[3, g, k], where(v))
            for k, v in enumerate(peers)
        ]

    steps = {"m": multiply, "f": first_send, "s": second_send, "t": third_send, "q": fourth_send}
    state = {"rows0": a}

    def round_step(name, k, inside):
        if name == "gram":
            if k == 1:
                state["rows1"] = dot_lanes(a, state["inverse0"], HIGHEST)
            state["sent"] = gram_send(k, state["rows%d" % k])
        elif name == "share":
            state["sent"] = gram_share(k, state["sent"])
        elif name == "take":
            state["gram"] = gram_take(k, state["sent"])
        else:
            state["inverse%d" % k] = cholesky_inverse(work, state["gram"], inside)

    for word in " ".join(PLAN).split():
        word, _, hooks = word.partition(":")

        def inside(strip, hooks=hooks):
            for hook in hooks.split(","):
                when, _, step = hook.partition("=")
                if when == str(strip):
                    steps[step[0]](int(step[1]))

        if word[0] in steps and len(word) == 2:
            steps[word[0]](int(word[1]))
        else:
            round_step(word[:-1], int(word[-1]) - 1, inside)
    second_left, inverse_one, inverse_two = state["rows1"], state["inverse0"], state["inverse1"]
    turn = dot(inverse_two, inverse_one, HIGHEST)
    basis = dot_lanes(second_left, inverse_two, HIGHEST)
    left_basis[...] = basis
    q12 = jnp.concatenate(split2(basis * (1.0 - momentum_decay)), axis=1)
    gathers = [copy for g in range(len(GROUPS)) for copy in moves[3, g]]
    for copy in sent:
        if not any(copy is gather for gather in gathers):
            copy.wait_send()
    t1, t2, t3 = split3(turn)
    t12 = jnp.concatenate([t1, t2], axis=1)
    t13 = jnp.concatenate([t1, t3], axis=1)
    energy = jnp.zeros((RANK, RANK), f32)
    for g, (start, size, _, _) in enumerate(GROUPS):
        for copy in moves[3, g]:
            copy.wait_recv()
        for at, width in tiles(size):
            cols = pl.ds(start + at, width)
            r1, r2, r3 = split3(rt[:, cols])
            right = dot(t12, jnp.concatenate([r1, r1], axis=0)) + (
                dot(t12, jnp.concatenate([r2, r2], axis=0)) + dot(t13, jnp.concatenate([r3, r1], axis=0))
            )
            right_rows[:, cols] = right
            for lane in range(0, width, RANK):
                tile = right[:, lane : lane + RANK]
                energy = energy + tile * tile
    squares[t] = dot_lanes(jnp.ones((8, RANK), f32), energy, HIGHEST)
    last = [
        remote(squares.at[t], squares.at[t], a_send.at[5 * CHUNKS + n], a_recv.at[5 * CHUNKS + n], peer)
        for n, peer in enumerate(t_peers)
    ]
    for n, (start, size, _, _) in enumerate(GROUPS):
        for at, width in tiles(size):
            cols = pl.ds(start + at, width)
            right = right_rows[:, cols]
            rounded = right.astype(bf16)
            summed[:, cols] = summed[:, cols] - dot(q12, jnp.concatenate([rounded, rounded], axis=0))
            new_factor[cols, :] = right.T
    for copy in gathers:
        copy.wait_send()
    for copy in last:
        copy.wait_recv()
    total = squares[0]
    for n in range(1, TENSOR):
        total = total + squares[n]
    new_factor[...] = new_factor[...] * lax.rsqrt(total[:1] + 1e-06)
    for copy in last:
        copy.wait_send()


def write_out(*refs):
    copies = []
    for source, target, pieces in zip(refs[:3], refs[3:6], PIECES):
        size = source.shape[0] // pieces
        for k in range(pieces):
            rows = pl.ds(k * size, size)
            copies.append(pltpu.make_async_copy(source.at[rows], target.at[rows], refs[6].at[len(copies)]))
            copies[-1].start()
    for copy in copies:
        copy.wait()


def per_device(momentum, gradient, factor):
    dma = pltpu.SemaphoreType.DMA
    results = pl.pallas_call(
        kernel,
        out_shape=(
            pltpu.VMEM((ROWS, COLS), f32),
            pltpu.VMEM((ROWS, RANK), f32),
            pltpu.VMEM((COLS, RANK), f32),
        ),
        in_specs=[pl.BlockSpec(memory_space=pltpu.HBM)] * 3,
        out_specs=[pl.BlockSpec(memory_space=pltpu.VMEM)] * 3,
        scratch_shapes=[
            pltpu.VMEM((ROWS, COLS), bf16),
            pltpu.VMEM((COLS, RANK), f32),
            pltpu.VMEM((ROWS, COLS), bf16),
            pltpu.VMEM((ROWS, COLS), bf16),
            pltpu.VMEM((ROWS, COLS), bf16),
            pltpu.VMEM((COLS, 2 * RANK), bf16),
            pltpu.VMEM((COLS, RANK), bf16),
            pltpu.VMEM((CHUNKS, CHUNK, RANK), f32),
            pltpu.VMEM((CHUNKS, CHUNK // 2, RANK), f32),
            pltpu.VMEM((CHUNKS, SIDE, CHUNK // 2, RANK), f32),
            pltpu.VMEM((ROWS, RANK), f32),
            pltpu.VMEM((2, FSDP, RANK // TENSOR, RANK), f32),
            pltpu.VMEM((2, TENSOR, RANK // TENSOR, RANK), f32),
            pltpu.VMEM((RANK, RANK), f32),
            pltpu.VMEM((RANK, 2 * RANK), f32),
            pltpu.VMEM((RANK, COLS), f32),
            pltpu.VMEM((RANK, COLS), f32),
            pltpu.VMEM((SIDE - 1, RANK // SIDE, COLS), f32),
            pltpu.VMEM((SIDE - 1, RANK // FSDP, COLS), f32),
            pltpu.VMEM((TENSOR, 8, RANK), f32),
            pltpu.VMEM((RANK, COLS), f32),
            dma((2 * CHUNKS + 1,)),
            dma((5 * CHUNKS + TENSOR - 1,)),
            dma((5 * CHUNKS + TENSOR - 1,)),
            dma((2, FSDP + TENSOR - 2)),
            dma((2, FSDP + TENSOR - 2)),
            dma((4, len(GROUPS), SIDE - 1)),
            dma((4, len(GROUPS), SIDE - 1)),
        ],
        compiler_params=pltpu.CompilerParams(collective_id=0, has_side_effects=True, vmem_limit_bytes=44 << 20),
        cost_estimate=pl.CostEstimate(flops=8 * 10**9, bytes_accessed=20 * 10**6, transcendentals=0),
        name="dion_update",
    )(*(pltpu.with_memory_space_constraint(v, pltpu.HBM) for v in (momentum, gradient, factor)))
    return pl.pallas_call(
        write_out,
        out_shape=tuple(jax.ShapeDtypeStruct(v.shape, v.dtype) for v in results),
        in_specs=[pl.BlockSpec(memory_space=pl.ANY)] * 3,
        out_specs=[pl.BlockSpec(memory_space=pl.ANY)] * 3,
        scratch_shapes=[dma((sum(PIECES),))],
        compiler_params=pltpu.CompilerParams(vmem_limit_bytes=1 << 20),
        cost_estimate=pl.CostEstimate(flops=0, bytes_accessed=9 * 10**6, transcendentals=0),
        name="write_out",
    )(*(pltpu.with_memory_space_constraint(v, pltpu.VMEM) for v in results))


def solution(mesh):
    return jax.shard_map(
        per_device,
        mesh=mesh,
        in_specs=(P("fsdp", "tensor"), P("fsdp", "tensor"), P("tensor", None)),
        out_specs=(P("fsdp", "tensor"), P("fsdp", None), P("tensor", None)),
        check_vma=False,
    )
```
